256 devices in a mesh: band: 16 (over z, core), fft: 16 (over y, x).
Axes of the slice: x: 4, y: 4, z: 8, core: 2. Of those that a mesh axis runs over, the one named last changes fastest.
Arguments:
- wave_coeffs: bfloat16 [64, 96, 18432], P('band', 'fft'), may hold values from -128 to 128
- local_potential: float32 [192, 36864], P('fft'), may hold values from -1 to 1
- projector: bfloat16 [2048, 8, 1536], P('fft'), may hold values from -0.5 to 0.5
- slot_block: int32 [2048], P('fft'), may hold values from 0 to 287
- slot_atom: int32 [2048], P('fft'), may hold values from 0 to 999
- atom_species: int32 [1000], replicated, may hold values from 0 to 3
- proj_count: int32 [4], replicated, may hold values from 4 to 8
- projector_strength: float32 [4, 8, 8], replicated, may hold values from -3 to 3
Outputs:
- result_coeffs: bfloat16 [64, 96, 18432], P('band', 'fft')
- subspace: float32 [64, 4, 64], P('band')
The draws below stay inside these ranges and needn't reach their ends.
All inputs are finite; a program needn't handle non-finite values.
Results may differ from the reference program's by a relative error of at most 0.015.
Values may be sent and summed in bfloat16 or wider, within the bound.
No kernel may reach another device: no remote copies, remote signals or barrier semaphores. Data moves between devices by JAX's collectives and lax.ppermute only.
A program may use at most 128 MiB of HBM per device.

```python
import math
import jax
import jax.numpy as jnp
from jax import lax

NG = 192
KB = 96
NPROJ = 8
NSPEC = 4
NATOM = 1000
SLOTS_DEV = 128
NB = 64
SLOTS = 2048
XDEV = 12
BLOCK = 1536


def draw_wave_coeffs(key, part):
    key = jax.random.fold_in(key, 11)
    subkeys = jax.random.split(key, 6)
    field_count = 8
    shell_width = 1.0 + KB / 48.0
    signed = (jnp.arange(KB, dtype=jnp.int32) - KB // 2).astype(jnp.float32)
    squared = signed * signed
    radius = jnp.sqrt(squared[:, None, None] + squared[None, :, None] + squared[None, None, :])
    bright = jax.random.uniform(subkeys[0], (KB, 1, KB, KB), jnp.float32)
    brightness = 0.03 + jnp.exp(40.0 * (bright - 1.0))
    shell_radii = jax.random.uniform(subkeys[1], (field_count,), jnp.float32, minval=0.15 * KB, maxval=0.48 * KB)
    amplitude = jax.random.uniform(subkeys[2], (NB, 1, 1, 1, 1), jnp.float32, minval=0.4, maxval=1.0)
    coupling = jax.random.normal(subkeys[3], (2, field_count, NB), jnp.float32) * (0.5 / field_count) ** 0.5
    field_scale = (20.5 * KB / shell_width) ** 0.5
    noise_scale = 2.24
    fields = jax.random.normal(subkeys[4], (field_count, 2, KB, KB, KB), jnp.float32)
    noise_part = jax.random.normal(subkeys[5], (NB, KB, 2, KB, KB), jnp.float32)
    real_sum = jnp.zeros((NB, KB, KB, KB), jnp.float32)
    imag_sum = jnp.zeros((NB, KB, KB, KB), jnp.float32)
    for member in range(field_count):
        offset = radius - shell_radii[member]
        envelope = jnp.exp(-(offset * offset) / (2.0 * shell_width * shell_width)) * (KB / (4.0 * shell_radii[member]))
        field_real = (fields[member, 0] * envelope)[None]
        field_imag = (fields[member, 1] * envelope)[None]
        weight_real = coupling[0, member][:, None, None, None]
        weight_imag = coupling[1, member][:, None, None, None]
        real_sum = real_sum + weight_real * field_real - weight_imag * field_imag
        imag_sum = imag_sum + weight_real * field_imag + weight_imag * field_real
    shared = jnp.stack([real_sum, imag_sum], axis=2)
    values = amplitude * brightness[None] * (field_scale * shared + noise_scale * noise_part)
    values = jnp.clip(values, -128.0, 128.0)
    return values.reshape(NB, KB, 2 * KB * KB).astype(jnp.bfloat16)


def set_ends(values, rng, least, largest):
    extent = values.shape
    spot = [jax.random.randint(jax.random.fold_in(rng, axis), (), 0, extent[axis]) for axis in range(len(extent))]
    values = values.at[tuple(spot)].set(least)
    longest = extent.index(max(extent))
    spot[longest] = (spot[longest] + 1) % extent[longest]
    return values.at[tuple(spot)].set(largest)


def steps_of(own_key, extent, pieces, smallest, largest):
    def one(dim, shards_of):
        draws = jax.random.uniform(jax.random.fold_in(jax.random.fold_in(own_key, 6), dim), (shards_of,), jnp.float32, smallest / len(pieces), largest / len(pieces))
        return jnp.repeat(jnp.exp(draws), extent[dim] // shards_of).reshape((-1,) + (1,) * (len(extent) - dim - 1))

    loudness = one(*pieces[0])
    for cut in pieces[1:]:
        loudness = loudness * one(*cut)
    return loudness


def noise(key, shape, deviation, most, cuts=(), held_as=jnp.bfloat16):
    array = jax.random.normal(key, shape, jnp.float32) * deviation
    if len(cuts) > 0:
        array = steps_of(key, shape, cuts, -0.22, 0.18) * array
    return jnp.clip(array, min=-most, max=most).astype(held_as)


def setup_inputs(seed: int = 0) -> dict:
    key_list = jax.random.split(jax.random.key(seed), 9)
    wave_coeffs = draw_wave_coeffs(jax.random.fold_in(key_list[8], 71), 0)
    local_potential = jnp.clip(jax.random.uniform(key_list[1], (NG, NG * NG), jnp.float32, -1.0, 1.0) * steps_of(key_list[1], (NG, NG * NG), ((0, 16),), -0.4, 0.0), -1.0, 1.0)
    projector = noise(key_list[2], (SLOTS, NPROJ, BLOCK), 128 ** -0.5, 0.5, ((0, 16),))
    slot_block = set_ends(jax.random.randint(key_list[3], (SLOTS,), 0, XDEV * NG // 8), jax.random.fold_in(key_list[3], 1), 0, (XDEV * NG // 8) - 1).astype(jnp.int32)
    slot_atom = set_ends(jax.random.randint(key_list[4], (SLOTS,), 0, NATOM), jax.random.fold_in(key_list[4], 1), 0, NATOM - 1).astype(jnp.int32)
    atom_species = set_ends(jax.random.randint(key_list[5], (NATOM,), 0, NSPEC), jax.random.fold_in(key_list[5], 1), 0, NSPEC - 1).astype(jnp.int32)
    proj_count = set_ends(jax.random.randint(key_list[6], (NSPEC,), NPROJ // 2, NPROJ + 1), jax.random.fold_in(key_list[6], 1), NPROJ // 2, NPROJ).astype(jnp.int32)
    projector_strength = noise(key_list[7], (NSPEC, NPROJ, NPROJ), 0.5, 3.0, (), jnp.float32)
    return {"wave_coeffs": wave_coeffs, "local_potential": local_potential, "projector": projector, "slot_block": slot_block, "slot_atom": slot_atom, "atom_species": atom_species, "proj_count": proj_count, "projector_strength": projector_strength}


def make_table(amount, length, scaling, direction):
    frequency = jnp.arange(amount, dtype=jnp.int32) - amount // 2
    position = jnp.arange(length, dtype=jnp.int32)
    phases = frequency[:, None] * position[None, :] % length
    radians = phases.astype(jnp.float32) * (2.0 * math.pi / length)
    cosine = jnp.cos(radians) / math.sqrt(scaling)
    sine_part = direction * jnp.sin(radians) / math.sqrt(scaling)
    return jnp.stack([jnp.stack([cosine, sine_part]), jnp.stack([-sine_part, cosine])]).astype(jnp.bfloat16)

def contract(formula, values, weights_table):
    return jnp.einsum(formula, values.astype(jnp.float32), weights_table.astype(jnp.float32))

def atom_matrices(atom_species, proj_count, projector_strength):
    symmetric = 0.5 * (projector_strength + jnp.swapaxes(projector_strength, 1, 2))
    channel = jnp.arange(NPROJ, dtype=jnp.int32)
    active = (channel[None, :] < proj_count[:, None]).astype(jnp.float32)
    masked = symmetric * active[:, :, None] * active[:, None, :]
    species_hot = (atom_species[:, None] == jnp.arange(NSPEC, dtype=jnp.int32)[None, :]).astype(jnp.float32)
    return jnp.einsum('at,tpq->apq', species_hot, masked, precision=lax.Precision.HIGHEST)

def intersections(left_side, right_side):
    products = jnp.einsum('jkhdm,ihcm->jkdci', right_side.astype(jnp.float32), left_side.astype(jnp.float32))
    real_part = products[:, :, 0, 0] + products[:, :, 1, 1]
    imag_part = products[:, :, 1, 0] - products[:, :, 0, 1]
    stacked = jnp.stack([real_part, imag_part], axis=2)
    return stacked.reshape(stacked.shape[0], 4, stacked.shape[3])

def reference(wave_coeffs, local_potential, projector, slot_block, slot_atom, atom_species, proj_count, projector_strength):
    inverse = make_table(KB, NG, KB, 1.0)
    forward = make_table(KB, NG, NG, -1.0)
    holder = jnp.arange(SLOTS, dtype=jnp.int32) // SLOTS_DEV
    global_block = holder * (XDEV * NG // 8) + slot_block
    atom_matrix = atom_matrices(atom_species, proj_count, projector_strength)
    potential = local_potential.reshape(NG * NG // 8, 8 * NG)
    signed = (jnp.arange(KB, dtype=jnp.int32) - KB // 2).astype(jnp.float32)
    squares = signed * signed
    energy = 2.0 * (squares[:, None, None] + squares[None, :, None] + squares[None, None, :]) / (KB * KB)

    def one_band(spectra_band):
        spectra = spectra_band.reshape(KB, 2, KB, KB)
        section_x = contract('hcfg,cdfx->hdxg', spectra, inverse).astype(jnp.bfloat16)
        section_y = contract('hcxg,cdgy->hdxy', section_x, inverse).astype(jnp.bfloat16)
        real_space = contract('hcxy,cdhz->dxyz', section_y, inverse).astype(jnp.bfloat16)
        blocks = real_space.reshape(2, NG * NG // 8, 8 * NG)
        gathered = blocks[:, global_block]
        slot_terms = contract('spn,csn->spc', projector, gathered)
        coefficients = jax.ops.segment_sum(slot_terms, slot_atom, num_segments=NATOM)
        weighted = jnp.einsum('apq,aqc->apc', atom_matrix, coefficients, precision=lax.Precision.HIGHEST).astype(jnp.bfloat16)
        slot_weights = weighted[slot_atom]
        nonlocal_part = contract('spn,spc->csn', projector, slot_weights)
        nonlocal_sum = jnp.zeros((2, NG * NG // 8, 8 * NG), jnp.float32).at[:, global_block].add(nonlocal_part)
        applied = (potential[None] * blocks.astype(jnp.float32) + nonlocal_sum).astype(jnp.bfloat16)
        applied = applied.reshape(2, NG, NG, NG)
        back_z = contract('cxyz,cdhz->dxyh', applied, forward).astype(jnp.bfloat16)
        back_y = contract('cxyh,cdgy->dxgh', back_z, forward).astype(jnp.bfloat16)
        spectrum = contract('cxgh,cdfx->hdfg', back_y, forward)
        result = spectrum + energy[:, None, :, :] * spectra.astype(jnp.float32)
        return result.astype(jnp.bfloat16).reshape(KB, 2 * KB * KB)
    result_coeffs = lax.map(one_band, wave_coeffs)
    left_side = wave_coeffs.reshape(NB, KB, 2, KB * KB)
    right_side = jnp.stack([wave_coeffs, result_coeffs], axis=1).reshape(NB, 2, KB, 2, KB * KB)
    subspace = intersections(left_side, right_side) * (1.0 / (KB * KB * KB))
    return (result_coeffs, subspace)
```

```python
import math

import jax
import jax.numpy as jnp
import ml_dtypes
import numpy as np
from jax import lax
from jax.experimental import pallas as pl
from jax.experimental.pallas import tpu as pltpu
from jax.sharding import PartitionSpec as P

NG = 192
KB = 96
NPROJ = 8
NSPEC = 4
ND = 16
XD = NG // ND
HD = KB // ND
NBD = 4
SD = 128
NBLK = XD * NG // 8
DX = 2 * XD
LANES = HD * NBD * KB
TILES = LANES // 128
GROUP = NBD * KB
PLANE = 2 * KB * KB
BF = jnp.bfloat16
F32 = jnp.float32
HIGH = lax.Precision.HIGHEST
MIB = 1024 * 1024
PLANE_UNROLL = 2


def table(scaling, direction):
    phases = ((np.arange(KB) - KB // 2)[:, None] * np.arange(NG)[None, :]) % NG
    radians = phases.astype(np.float64) * (2.0 * math.pi / NG)
    cosine = np.cos(radians) / math.sqrt(scaling)
    sine = direction * np.sin(radians) / math.sqrt(scaling)
    full = np.stack([np.stack([cosine, sine]), np.stack([-sine, cosine])])
    return full.astype(np.float32).astype(ml_dtypes.bfloat16)


def pad_last(array, width):
    return np.pad(array, [(0, 0)] * (array.ndim - 1) + [(0, width - array.shape[-1])])


def constants():
    inverse = table(KB, 1.0)
    forward = table(NG, -1.0)
    out = {}
    inv_x = inverse.reshape(2, 2, KB, ND, XD)
    out["a"] = inv_x.transpose(3, 1, 4, 0, 2).reshape(ND * DX, 2 * KB)
    real_part = pad_last(inverse[0, 0].T, 128)
    imag_part = pad_last(inverse[0, 1].T, 128)
    out["by"] = np.concatenate([real_part, imag_part], axis=1)
    inv_z = inverse.reshape(2, 2, ND, HD, NG).transpose(0, 3, 2, 1, 4)
    out["bz"] = pad_last(inv_z, 256).reshape(2 * KB, 512)
    fwd_z = forward.reshape(2, 2, ND, HD, NG).transpose(1, 3, 2, 0, 4)
    out["cz"] = pad_last(fwd_z, 256).reshape(2 * KB, 512)
    out["cy"] = pad_last(forward.transpose(0, 3, 1, 2), 128).reshape(2, NG, 256)
    fwd_x = forward.reshape(2, 2, KB, ND, XD)
    out["d"] = fwd_x.transpose(1, 2, 3, 0, 4).reshape(2 * KB, ND * DX)
    return out


def dot(left, right):
    return jnp.dot(left, right, preferred_element_type=F32)


def dot_nt(left, right):
    return lax.dot_general(left, right, (((1,), (1,)), ((), ())), preferred_element_type=F32)


def iota(shape, axis):
    return lax.broadcasted_iota(jnp.int32, shape, axis)


def x_kernel(table_ref, wave_ref, out_ref):
    for h in range(HD):
        parts = [
            jnp.concatenate([wave_ref[h, b].astype(F32), jnp.zeros((2 * KB, 32), F32)], axis=1)
            for b in range(NBD)
        ]
        right = jnp.concatenate(join_bands(parts), axis=1).astype(BF)
        out_ref[:, h * GROUP : (h + 1) * GROUP] = dot(table_ref[...], right).astype(BF)


def x_transform(table_x, wave):
    return pl.pallas_call(
        x_kernel,
        out_shape=jax.ShapeDtypeStruct((ND * DX, LANES), BF),
        compiler_params=pltpu.CompilerParams(vmem_limit_bytes=60 * MIB),
        name="x_transform",
    )(table_x, wave)


def split_bands(first, second, third):
    lane = iota(first.shape, 1)
    one = pltpu.roll(jnp.where(lane >= 96, first, second), 32, 1)
    two = pltpu.roll(jnp.where(lane >= 64, second, third), 64, 1)
    return first, one, two, pltpu.roll(third, 96, 1)


def join_bands(parts):
    lane = iota(parts[0].shape, 1)
    one = pltpu.roll(parts[1], 96, 1)
    two = pltpu.roll(parts[2], 64, 1)
    three = pltpu.roll(parts[3], 32, 1)
    return (
        jnp.where(lane < 96, parts[0], one),
        jnp.where(lane < 64, one, two),
        jnp.where(lane < 32, two, three),
    )


def grid_kernel(
    slot_ref, ty_ref, tz_ref, fold_ref, sums_ref, ids_ref, in_ref, proj_in_ref,
    exch_ref, real_ref,
    held_ref, proj_ref, wide_ref, space_ref, terms_ref, in_sems, proj_sem, out_sems,
):
    def columns_in(h):
        columns = pl.ds(h * GROUP, GROUP)
        return pltpu.make_async_copy(in_ref.at[:, columns], held_ref.at[h], in_sems.at[h])

    def plane_out(plane):
        blocks = pl.ds(plane * (NG // 8), NG // 8)
        return pltpu.make_async_copy(space_ref.at[blocks], real_ref.at[blocks], out_sems.at[plane])

    for h in range(HD):
        columns_in(h).start()
    projector_in = pltpu.make_async_copy(proj_in_ref, proj_ref, proj_sem)
    projector_in.start()
    for h in range(HD):
        columns_in(h).wait()
        for v in range(3):
            wide_ref[3 * h + v] = held_ref[h, :, v * 128 : v * 128 + 128].astype(F32)

    def plane_step(plane, carry):
        pieces = []
        for d in range(2):
            rows = pl.ds(d * XD + plane, ND, stride=DX)
            columns = [
                jnp.concatenate([wide_ref[3 * h + v, rows, :] for h in range(HD)], axis=0)
                for v in range(3)
            ]
            pieces.append(split_bands(*columns))
        section = []
        for b in range(NBD):
            real_part, imag_part = pieces[0][b], pieces[1][b]
            right = jnp.concatenate(
                [
                    jnp.concatenate([real_part, -imag_part], axis=1),
                    jnp.concatenate([imag_part, real_part], axis=1),
                ],
                axis=0,
            ).astype(BF)
            section.append(dot_nt(ty_ref[...], right).astype(BF))
        whole = dot(jnp.concatenate(section, axis=0), tz_ref[...])
        for b in range(NBD):
            cells = whole[NG * b : NG * b + NG]
            both = jnp.concatenate(
                [cells[:, :256].reshape(NG // 8, 8, 256), cells[:, 256:].reshape(NG // 8, 8, 256)],
                axis=1,
            ).astype(BF)
            space_ref[pl.ds(plane * (NG // 8), NG // 8), 16 * b : 16 * b + 16, :] = both
        plane_out(plane).start()
        return carry

    lax.fori_loop(0, XD, plane_step, 0, unroll=PLANE_UNROLL)
    projector_in.wait()
    lane = iota((8, 64), 1) % 8

    def slot(s, carry):
        cells = space_ref[slot_ref[s]]
        product = dot_nt(proj_ref[s], cells[:, :NG]).reshape(8, 8, 64)
        total = jnp.where(lane == 0, product[0], 0.0)
        for y in range(1, 8):
            total = jnp.where(lane == y, product[y], total)
        terms_ref[pl.ds(pl.multiple_of(s * 8, 8), 8), :] = total
        return carry

    lax.fori_loop(0, SD, slot, 0, unroll=8)
    terms = terms_ref[...]
    high = terms.astype(BF)
    low = (terms - high.astype(F32)).astype(BF)
    folded = dot(high, fold_ref[...]) + dot(low, fold_ref[...])
    keep = iota(folded.shape, 0) % 8 == iota(folded.shape, 1) % 64 // 8
    folded = jnp.where(keep, folded, 0.0).astype(BF)
    ordered = dot(sums_ref[...], folded)
    packed = jnp.where(iota((64, 128), 1) < 64, ordered[:64], ordered[64:]).astype(BF)
    for k in range(ND):
        exch_ref[k, 0:64, :] = packed
        exch_ref[k, 64:80, :] = ids_ref[...]
    for plane in range(XD):
        plane_out(plane).wait()


def grid_part(tables, received, projector, slot_block, ids):
    fold = np.zeros((64, 128), np.float32)
    for bc in range(8):
        for y in range(8):
            fold[bc * 8 + y, bc::8] = 1.0
    sums = (np.arange(1024)[None, :] // 8 == np.arange(128)[:, None]).astype(np.float32)
    vmem, anywhere = pl.BlockSpec(memory_space=pltpu.VMEM), pl.BlockSpec(memory_space=pl.ANY)
    return pl.pallas_call(
        grid_kernel,
        in_specs=[pl.BlockSpec(memory_space=pltpu.SMEM)] + [vmem] * 5 + [anywhere] * 2,
        out_specs=[vmem, anywhere],
        out_shape=[
            jax.ShapeDtypeStruct((ND, 80, 128), BF),
            jax.ShapeDtypeStruct((NBLK, 64, 256), BF),
        ],
        scratch_shapes=[
            pltpu.VMEM((HD, ND * DX, GROUP), BF),
            pltpu.VMEM((SD, 64, NG), BF),
            pltpu.VMEM((TILES, ND * DX, 128), F32),
            pltpu.VMEM((NBLK, 64, 256), BF),
            pltpu.VMEM((SD * 8, 64), F32),
            pltpu.SemaphoreType.DMA((HD,)),
            pltpu.SemaphoreType.DMA,
            pltpu.SemaphoreType.DMA((XD,)),
        ],
        compiler_params=pltpu.CompilerParams(vmem_limit_bytes=60 * MIB),
        name="grid_part",
    )(
        slot_block, tables["by"], tables["bz"], jnp.asarray(fold, BF), jnp.asarray(sums, BF), ids,
        received, projector,
    )


def apply_kernel(
    slot_ref, exch_ref, own_ref, kinds_ref, mix_ref, rep_ref, spread_ref, tz_ref, ty_ref,
    real_in_ref, pot_in_ref, proj_in_ref,
    out_ref,
    real_ref, pot_ref, proj_ref, field_ref, wide_ref, weight_ref, real_sems, pot_sems, proj_sem,
):
    def plane_in(plane):
        blocks = pl.ds(plane * (NG // 8), NG // 8)
        return (
            pltpu.make_async_copy(real_in_ref.at[blocks], real_ref.at[blocks], real_sems.at[plane]),
            pltpu.make_async_copy(pot_in_ref.at[blocks], pot_ref.at[blocks], pot_sems.at[plane]),
        )

    for plane in range(XD):
        for copy in plane_in(plane):
            copy.start()
    projector_in = pltpu.make_async_copy(proj_in_ref, proj_ref, proj_sem)
    projector_in.start()

    row, col = iota((128, 128), 0), iota((128, 128), 1)
    halves = (row < 64) == (col < 64)
    total = jnp.zeros((SD, 128), F32)
    for source in range(ND):
        ids = exch_ref[source, 64:80, :].astype(F32)
        atoms = ids[0:1] * 32.0 + ids[1:2]
        same = jnp.where(own_ref[...] == atoms, 1.0, 0.0).astype(BF)
        terms = exch_ref[source, 0:64, :].astype(F32)
        terms = jnp.where(halves, jnp.concatenate([terms, terms], axis=0), 0.0).astype(BF)
        total = total + dot(same, terms)
    total = total + pltpu.roll(total, 64, 1)
    mixed = jnp.dot(total, mix_ref[...], preferred_element_type=F32, precision=HIGH)
    mixed = mixed * kinds_ref[...]
    mixed = mixed[:, :128] + mixed[:, 128:]
    weighted = (mixed + pltpu.roll(mixed, 64, 1)).astype(BF)
    spread = dot(rep_ref[...], weighted)
    keep = iota(spread.shape, 0) % 8 == iota(spread.shape, 1) % 8
    spread = jnp.where(keep, spread, 0.0).astype(BF)
    weight_ref[...] = dot(spread, spread_ref[...])

    def potential_step(plane, carry):
        for copy in plane_in(plane):
            copy.wait()
        for yb in range(NG // 8):
            block = plane * (NG // 8) + yb
            cells = real_ref[block].astype(F32).reshape(8, 8, 256)
            values = pot_ref[block]
            values = jnp.concatenate([values, jnp.zeros((8, 64), F32)], axis=1)
            field_ref[block] = (cells * values[None]).reshape(64, 256)
        return carry

    lax.fori_loop(0, XD, potential_step, 0)
    projector_in.wait()
    own = (iota((8, 64), 1) // 8 == iota((8, 64), 0)).astype(F32)

    def slot(s, carry):
        rows = weight_ref[pl.ds(pl.multiple_of(s * 8, 8), 8), :]
        matrix = (rows[:, None, :] * own[None]).reshape(64, 64).astype(BF)
        block = slot_ref[s]
        field_ref[block, :, :NG] = field_ref[block, :, :NG] + dot(matrix, proj_ref[s])
        return carry

    lax.fori_loop(0, SD, slot, 0, unroll=8)

    def plane_step(plane, carry):
        start = plane * (NG // 8)
        parts = []
        for b in range(NBD):
            zero = field_ref[pl.ds(start, NG // 8), 16 * b : 16 * b + 8, :].reshape(NG, 256)
            one = field_ref[pl.ds(start, NG // 8), 16 * b + 8 : 16 * b + 16, :].reshape(NG, 256)
            cells = jnp.concatenate([zero, one], axis=1).astype(BF)
            parts.append(dot_nt(tz_ref[...], cells).astype(BF))
        both = dot(jnp.concatenate([part[:KB] for part in parts], axis=0), ty_ref[0])
        both = both + dot(jnp.concatenate([part[KB:] for part in parts], axis=0), ty_ref[1])
        for d in range(2):
            joined = join_bands(
                [both[KB * b : KB * b + KB, 128 * d : 128 * d + 128] for b in range(NBD)]
            )
            rows = pl.ds(d * XD + plane, ND, stride=DX)
            for h in range(HD):
                for v in range(3):
                    wide_ref[3 * h + v, rows, :] = joined[v][16 * h : 16 * h + 16]
        return carry

    lax.fori_loop(0, XD, plane_step, 0, unroll=PLANE_UNROLL)
    for t in range(TILES):
        out_ref[:, t * 128 : t * 128 + 128] = wide_ref[t].astype(BF)


def apply_part(tables, exchanged, own, kinds, mix, real_space, potential, projector, slot_block):
    rep = (np.arange(1024)[:, None] // 8 == np.arange(128)[None, :]).astype(np.float32)
    spread = np.zeros((128, 64), np.float32)
    for p in range(8):
        spread[p * 8 : p * 8 + 8, p::8] = 1.0
    vmem, anywhere = pl.BlockSpec(memory_space=pltpu.VMEM), pl.BlockSpec(memory_space=pl.ANY)
    return pl.pallas_call(
        apply_kernel,
        in_specs=[pl.BlockSpec(memory_space=pltpu.SMEM)] + [vmem] * 8 + [anywhere] * 3,
        out_specs=vmem,
        out_shape=jax.ShapeDtypeStruct((ND * DX, LANES), BF),
        scratch_shapes=[
            pltpu.VMEM((NBLK, 64, 256), BF),
            pltpu.VMEM((NBLK, 8, NG), F32),
            pltpu.VMEM((SD, 64, NG), BF),
            pltpu.VMEM((NBLK, 64, 256), F32),
            pltpu.VMEM((TILES, ND * DX, 128), F32),
            pltpu.VMEM((SD * 8, 64), F32),
            pltpu.SemaphoreType.DMA((XD,)),
            pltpu.SemaphoreType.DMA((XD,)),
            pltpu.SemaphoreType.DMA,
        ],
        compiler_params=pltpu.CompilerParams(vmem_limit_bytes=60 * MIB),
        name="apply_part",
    )(
        slot_block, exchanged, own, kinds, mix, jnp.asarray(rep, BF), jnp.asarray(spread, BF),
        tables["cz"], tables["cy"], real_space, potential, projector,
    )


def back_kernel(kz_ref, table_ref, in_ref, wave_ref, squares_ref, out_ref):
    for h in range(HD):
        kz = (kz_ref[0] + (h - KB // 2)).astype(F32)
        energy = (squares_ref[...] + kz * kz) * (2.0 / (KB * KB))
        spectrum = dot(table_ref[...], in_ref[:, h * GROUP : (h + 1) * GROUP])
        parts = split_bands(spectrum[:, :128], spectrum[:, 128:256], spectrum[:, 256:])
        for b in range(NBD):
            own = wave_ref[h, b].astype(F32)
            out_ref[h, b] = (parts[b][:, :KB] + energy * own).astype(BF)


def back_transform(table_x, first_kz, received, wave):
    signed = np.arange(KB) - KB // 2
    squares = (signed * signed)[:, None] + (signed * signed)[None, :]
    squares = np.tile(squares, (2, 1)).astype(np.float32)
    return pl.pallas_call(
        back_kernel,
        in_specs=[pl.BlockSpec(memory_space=pltpu.SMEM)]
        + [pl.BlockSpec(memory_space=pltpu.VMEM)] * 4,
        out_shape=jax.ShapeDtypeStruct((HD, NBD, 2 * KB, KB), BF),
        compiler_params=pltpu.CompilerParams(vmem_limit_bytes=60 * MIB),
        name="back_transform",
    )(first_kz, table_x, received, wave, jnp.asarray(squares))


ROWS = HD * NBD
CHUNK = 2304
CHUNKS = KB * KB // CHUNK


def subspace_kernel(
    all0_ref, all1_ref, wave0_ref, wave1_ref, result0_ref, result1_ref,
    fold0_ref, fold1_ref, rows_ref,
    out_ref,
    acc0, acc1,
):
    step = pl.program_id(0)

    @pl.when(step == 0)
    def _():
        acc0[...] = jnp.zeros_like(acc0)
        acc1[...] = jnp.zeros_like(acc1)

    own = [wave0_ref, result0_ref, wave1_ref, result1_ref]
    right = jnp.concatenate([ref[...].astype(F32) for ref in own], axis=0).astype(BF)
    acc0[...] += dot_nt(all0_ref[...], right)
    acc1[...] += dot_nt(all1_ref[...], right)

    @pl.when(step == CHUNKS - 1)
    def _():
        shape = acc0.shape
        keep = iota(shape, 0) % ROWS // NBD == iota(shape, 1) % ROWS // NBD
        folded = jnp.dot(
            jnp.where(keep, acc0[...], 0.0), fold0_ref[...], precision=HIGH
        ) + jnp.dot(jnp.where(keep, acc1[...], 0.0), fold1_ref[...], precision=HIGH)
        turned = jnp.dot(folded.T[:16], rows_ref[...], precision=HIGH)
        packed = jnp.where(iota((8, 128), 1) < 64, turned[:8], turned[8:])
        for k in range(ND):
            out_ref[k] = packed


def subspace_part(everything, wave, result):
    fold0 = np.zeros((2, 2, HD, NBD, 128), np.float32)
    fold1 = np.zeros((2, 2, HD, NBD, 128), np.float32)
    for k in range(2):
        for j in range(NBD):
            fold0[0, k, :, j, 4 * j + 2 * k] = 1.0
            fold0[1, k, :, j, 4 * j + 2 * k + 1] = 1.0
            fold1[1, k, :, j, 4 * j + 2 * k] = 1.0
            fold1[0, k, :, j, 4 * j + 2 * k + 1] = -1.0
    total = everything.shape[0]
    row = np.arange(total)
    band = row // ROWS * NBD + row % NBD
    rows = (band[:, None] == np.arange(128)[None, :] % 64).astype(np.float32)
    whole = lambda *shape: pl.BlockSpec(shape, lambda i: (0,) * len(shape))
    return pl.pallas_call(
        subspace_kernel,
        grid=(CHUNKS,),
        in_specs=[
            pl.BlockSpec((total, CHUNK), lambda i: (0, i)),
            pl.BlockSpec((total, CHUNK), lambda i: (0, CHUNKS + i)),
            pl.BlockSpec((ROWS, CHUNK), lambda i: (0, i)),
            pl.BlockSpec((ROWS, CHUNK), lambda i: (0, CHUNKS + i)),
            pl.BlockSpec((ROWS, CHUNK), lambda i: (0, i)),
            pl.BlockSpec((ROWS, CHUNK), lambda i: (0, CHUNKS + i)),
            whole(4 * ROWS, 128),
            whole(4 * ROWS, 128),
            whole(total, 128),
        ],
        out_specs=whole(ND, 8, 128),
        out_shape=jax.ShapeDtypeStruct((ND, 8, 128), F32),
        scratch_shapes=[pltpu.VMEM((total, 4 * ROWS), F32), pltpu.VMEM((total, 4 * ROWS), F32)],
        compiler_params=pltpu.CompilerParams(vmem_limit_bytes=60 * MIB),
        name="subspace_part",
    )(
        everything, everything, wave, wave, result, result,
        jnp.asarray(fold0.reshape(-1, 128)), jnp.asarray(fold1.reshape(-1, 128)), jnp.asarray(rows),
    )


def exchange(array):
    return lax.all_to_all(array, "fft", split_axis=0, concat_axis=0, tiled=True)


def on_device(
    wave_coeffs,
    local_potential,
    projector,
    slot_block,
    slot_atom,
    atom_species,
    proj_count,
    projector_strength,
):
    tables = {name: jnp.asarray(value) for name, value in constants().items()}
    rows = wave_coeffs.transpose(1, 0, 2)
    wave = rows.reshape(HD, NBD, 2 * KB, KB)
    projector = projector.reshape(SD, NPROJ, 8, NG).transpose(0, 2, 1, 3).reshape(SD, 64, NG)
    potential = local_potential.reshape(NBLK, 8, NG)
    ids = jnp.concatenate(
        [(slot_atom // 32)[None], (slot_atom % 32)[None], jnp.zeros((14, SD), jnp.int32)]
    ).astype(BF)
    own_ids = jnp.broadcast_to(slot_atom.astype(F32)[:, None], (SD, 128))
    species = jnp.take(atom_species, slot_atom, axis=0)
    kinds = (species[:, None] == jnp.arange(256, dtype=jnp.int32)[None, :] // 64).astype(F32)
    symmetric = 0.5 * (projector_strength + jnp.swapaxes(projector_strength, 1, 2))
    active = (jnp.arange(NPROJ, dtype=jnp.int32)[None, :] < proj_count[:, None]).astype(F32)
    masked = symmetric * active[:, :, None] * active[:, None, :]
    mix = masked.transpose(2, 0, 1)[:, None, :, :, None] * jnp.eye(8, dtype=F32)[None, :, None, None]
    mix = jnp.pad(mix.reshape(64, 256), ((0, 64), (0, 0)))

    sent = x_transform(tables["a"], wave)
    sent, rows = lax.optimization_barrier((sent, rows))
    flat = rows.reshape(ROWS, PLANE)
    everything = lax.all_gather(flat, "band", axis=0, tiled=True)
    received = exchange(sent.reshape(ND, DX, LANES)).reshape(ND * DX, LANES)
    terms, real_space = grid_part(tables, received, projector, slot_block, ids)
    exchanged = exchange(terms)
    sent = apply_part(
        tables, exchanged, own_ids, kinds, mix, real_space, potential, projector, slot_block
    )
    received = exchange(sent.reshape(ND, DX, LANES)).reshape(ND * DX, LANES)
    first_kz = (lax.axis_index("fft") * HD).astype(jnp.int32).reshape(1)
    result = back_transform(tables["d"], first_kz, received, wave)
    result = result.reshape(ROWS, PLANE)
    partial = subspace_part(everything, flat, result)
    summed = exchange(partial).sum(axis=0) * (1.0 / (KB * KB * KB))
    subspace = summed.reshape(8, 2, 64).transpose(1, 0, 2).reshape(NBD, 4, 64)
    result_coeffs = result.reshape(HD, NBD, PLANE).transpose(1, 0, 2)
    return (result_coeffs, subspace)


def solution(mesh):
    return jax.shard_map(
        on_device,
        mesh=mesh,
        in_specs=(
            P("band", "fft", None),
            P("fft", None),
            P("fft", None, None),
            P("fft"),
            P("fft"),
            P(),
            P(),
            P(),
        ),
        out_specs=(P("band", "fft", None), P("band", None, None)),
        check_vma=False,
    )
```

```python
import math

import jax
import jax.numpy as jnp
import ml_dtypes
import numpy as np
from jax import lax
from jax.experimental import pallas as pl
from jax.experimental.pallas import tpu as pltpu
from jax.sharding import PartitionSpec as P

NG = 192
KB = 96
NPROJ = 8
NSPEC = 4
ND = 16
XD = NG // ND
HD = KB // ND
NBD = 4
SD = 128
NBLK = XD * NG // 8
DX = 2 * XD
LANES = HD * NBD * KB
TILES = LANES // 128
GROUP = NBD * KB
PLANE = 2 * KB * KB
BF = jnp.bfloat16
F32 = jnp.float32
HIGH = lax.Precision.HIGHEST
MIB = 1024 * 1024
PLANE_UNROLL = 3


def table(scaling, direction):
    phases = ((np.arange(KB) - KB // 2)[:, None] * np.arange(NG)[None, :]) % NG
    radians = phases.astype(np.float64) * (2.0 * math.pi / NG)
    cosine = np.cos(radians) / math.sqrt(scaling)
    sine = direction * np.sin(radians) / math.sqrt(scaling)
    full = np.stack([np.stack([cosine, sine]), np.stack([-sine, cosine])])
    return full.astype(np.float32).astype(ml_dtypes.bfloat16)


def pad_last(array, width):
    return np.pad(array, [(0, 0)] * (array.ndim - 1) + [(0, width - array.shape[-1])])


def constants():
    inverse = table(KB, 1.0)
    forward = table(NG, -1.0)
    out = {}
    inv_x = inverse.reshape(2, 2, KB, ND, XD)
    out["a"] = inv_x.transpose(3, 1, 4, 0, 2).reshape(ND * DX, 2 * KB)
    real_part = pad_last(inverse[0, 0].T, 128)
    imag_part = pad_last(inverse[0, 1].T, 128)
    out["by"] = np.concatenate([real_part, imag_part], axis=1)
    inv_z = inverse.reshape(2, 2, ND, HD, NG).transpose(0, 3, 2, 1, 4)
    out["bz"] = pad_last(inv_z, 256).reshape(2 * KB, 512)
    fwd_z = forward.reshape(2, 2, ND, HD, NG).transpose(1, 3, 2, 0, 4)
    out["cz"] = pad_last(fwd_z, 256).reshape(2 * KB, 512)
    out["cy"] = pad_last(forward.transpose(0, 3, 1, 2), 128).reshape(2, NG, 256)
    fwd_x = forward.reshape(2, 2, KB, ND, XD)
    out["d"] = fwd_x.transpose(1, 2, 3, 0, 4).reshape(2 * KB, ND * DX)
    return out


def dot(left, right):
    return jnp.dot(left, right, preferred_element_type=F32)


def dot_nt(left, right):
    return lax.dot_general(left, right, (((1,), (1,)), ((), ())), preferred_element_type=F32)


def iota(shape, axis):
    return lax.broadcasted_iota(jnp.int32, shape, axis)


def x_kernel(table_ref, wave_ref, out_ref):
    for h in range(HD):
        parts = [
            jnp.concatenate([wave_ref[h, b].astype(F32), jnp.zeros((2 * KB, 32), F32)], axis=1)
            for b in range(NBD)
        ]
        right = jnp.concatenate(join_bands(parts), axis=1).astype(BF)
        out_ref[:, h * GROUP : (h + 1) * GROUP] = dot(table_ref[...], right).astype(BF)


def x_transform(table_x, wave):
    return pl.pallas_call(
        x_kernel,
        out_shape=jax.ShapeDtypeStruct((ND * DX, LANES), BF),
        compiler_params=pltpu.CompilerParams(vmem_limit_bytes=24 * MIB),
        name="x_transform",
    )(table_x, wave)


def split_bands(first, second, third):
    lane = iota(first.shape, 1)
    one = pltpu.roll(jnp.where(lane >= 96, first, second), 32, 1)
    two = pltpu.roll(jnp.where(lane >= 64, second, third), 64, 1)
    return first, one, two, pltpu.roll(third, 96, 1)


def join_bands(parts):
    lane = iota(parts[0].shape, 1)
    one = pltpu.roll(parts[1], 96, 1)
    two = pltpu.roll(parts[2], 64, 1)
    three = pltpu.roll(parts[3], 32, 1)
    return (
        jnp.where(lane < 96, parts[0], one),
        jnp.where(lane < 64, one, two),
        jnp.where(lane < 32, two, three),
    )


def grid_kernel(
    slot_ref, ty_ref, tz_ref, fold_ref, ids_ref, in_ref, proj_in_ref,
    exch_ref, real_ref,
    proj_ref, wide_ref, space_ref, terms_ref, proj_sem, out_sems,
):
    def plane_out(plane):
        blocks = pl.ds(plane * (NG // 8), NG // 8)
        return pltpu.make_async_copy(space_ref.at[blocks], real_ref.at[blocks], out_sems.at[plane])

    projector_in = pltpu.make_async_copy(proj_in_ref, proj_ref, proj_sem)
    projector_in.start()
    for t in range(TILES):
        wide_ref[t] = in_ref[:, t * 128 : t * 128 + 128].astype(F32)

    def plane_step(plane, carry):
        pieces = []
        for d in range(2):
            rows = pl.ds(d * XD + plane, ND, stride=DX)
            columns = [
                jnp.concatenate([wide_ref[3 * h + v, rows, :] for h in range(HD)], axis=0)
                for v in range(3)
            ]
            pieces.append(split_bands(*columns))
        section = []
        for b in range(NBD):
            real_part, imag_part = pieces[0][b], pieces[1][b]
            right = jnp.concatenate(
                [
                    jnp.concatenate([real_part, -imag_part], axis=1),
                    jnp.concatenate([imag_part, real_part], axis=1),
                ],
                axis=0,
            ).astype(BF)
            section.append(dot_nt(ty_ref[...], right).astype(BF))
        whole = dot(jnp.concatenate(section, axis=0), tz_ref[...])
        for b in range(NBD):
            cells = whole[NG * b : NG * b + NG]
            both = jnp.concatenate(
                [cells[:, :256].reshape(NG // 8, 8, 256), cells[:, 256:].reshape(NG // 8, 8, 256)],
                axis=1,
            ).astype(BF)
            space_ref[pl.ds(plane * (NG // 8), NG // 8), 16 * b : 16 * b + 16, :] = both
        plane_out(plane).start()
        return carry

    lax.fori_loop(0, XD, plane_step, 0, unroll=PLANE_UNROLL)
    projector_in.wait()
    lane = iota((8, 64), 1) % 8

    def slot(s, carry):
        cells = space_ref[slot_ref[s]]
        product = dot_nt(proj_ref[s], cells[:, :NG]).reshape(8, 8, 64)
        total = jnp.where(lane == 0, product[0], 0.0)
        for y in range(1, 8):
            total = jnp.where(lane == y, product[y], total)
        terms_ref[pl.ds(pl.multiple_of(s * 8, 8), 8), :] = total
        return carry

    lax.fori_loop(0, SD, slot, 0, unroll=8)
    terms = terms_ref[...]
    high = terms.astype(BF)
    low = (terms - high.astype(F32)).astype(BF)
    folded = dot(high, fold_ref[...]) + dot(low, fold_ref[...])
    keep = iota(folded.shape, 0) % 8 == iota(folded.shape, 1) % 64 // 8
    folded = jnp.where(keep, folded, 0.0).astype(BF)
    sums = jnp.where(iota((SD, 1024), 1) // 8 == iota((SD, 1024), 0), 1.0, 0.0).astype(BF)
    ordered = dot(sums, folded)
    packed = jnp.where(iota((64, 128), 1) < 64, ordered[:64], ordered[64:]).astype(BF)
    for k in range(ND):
        exch_ref[k, 0:64, :] = packed
        exch_ref[k, 64:80, :] = ids_ref[...]
    for plane in range(XD):
        plane_out(plane).wait()


def grid_part(tables, received, projector, slot_block, ids):
    fold = np.zeros((64, 128), np.float32)
    for bc in range(8):
        for y in range(8):
            fold[bc * 8 + y, bc::8] = 1.0
    vmem, anywhere = pl.BlockSpec(memory_space=pltpu.VMEM), pl.BlockSpec(memory_space=pl.ANY)
    return pl.pallas_call(
        grid_kernel,
        in_specs=[pl.BlockSpec(memory_space=pltpu.SMEM)] + [vmem] * 5 + [anywhere],
        out_specs=[vmem, anywhere],
        out_shape=[
            jax.ShapeDtypeStruct((ND, 80, 128), BF),
            jax.ShapeDtypeStruct((NBLK, 64, 256), BF),
        ],
        scratch_shapes=[
            pltpu.VMEM((SD, 64, NG), BF),
            pltpu.VMEM((TILES, ND * DX, 128), F32),
            pltpu.VMEM((NBLK, 64, 256), BF),
            pltpu.VMEM((SD * 8, 64), F32),
            pltpu.SemaphoreType.DMA,
            pltpu.SemaphoreType.DMA((XD,)),
        ],
        compiler_params=pltpu.CompilerParams(vmem_limit_bytes=58 * MIB),
        name="grid_part",
    )(
        slot_block, tables["by"], tables["bz"], jnp.asarray(fold, BF), ids,
        received, projector,
    )


def apply_kernel(
    slot_ref, exch_ref, own_ref, kinds_ref, mix_ref, spread_ref, tz_ref, ty_ref,
    real_in_ref, pot_in_ref, proj_in_ref,
    out_ref,
    real_ref, pot_ref, proj_ref, field_ref, wide_ref, weight_ref, real_sems, pot_sems, proj_sem,
):
    def plane_in(plane):
        blocks = pl.ds(plane * (NG // 8), NG // 8)
        return (
            pltpu.make_async_copy(real_in_ref.at[blocks], real_ref.at[blocks], real_sems.at[plane]),
            pltpu.make_async_copy(pot_in_ref.at[blocks], pot_ref.at[blocks], pot_sems.at[plane]),
        )

    for plane in range(XD):
        for copy in plane_in(plane):
            copy.start()
    projector_in = pltpu.make_async_copy(proj_in_ref, proj_ref, proj_sem)
    projector_in.start()

    row, col = iota((128, 128), 0), iota((128, 128), 1)
    halves = (row < 64) == (col < 64)
    total = jnp.zeros((SD, 128), F32)
    for source in range(ND):
        ids = exch_ref[source, 64:80, :].astype(F32)
        atoms = ids[0:1] * 32.0 + ids[1:2]
        same = jnp.where(own_ref[...] == atoms, 1.0, 0.0).astype(BF)
        terms = exch_ref[source, 0:64, :].astype(F32)
        terms = jnp.where(halves, jnp.concatenate([terms, terms], axis=0), 0.0).astype(BF)
        total = total + dot(same, terms)
    total = total + pltpu.roll(total, 64, 1)
    mixed = jnp.dot(total, mix_ref[...], preferred_element_type=F32, precision=HIGH)
    mixed = mixed * kinds_ref[...]
    mixed = mixed[:, :128] + mixed[:, 128:]
    weighted = (mixed + pltpu.roll(mixed, 64, 1)).astype(BF)
    repeat = jnp.where(iota((1024, SD), 0) // 8 == iota((1024, SD), 1), 1.0, 0.0).astype(BF)
    spread = dot(repeat, weighted)
    keep = iota(spread.shape, 0) % 8 == iota(spread.shape, 1) % 8
    spread = jnp.where(keep, spread, 0.0).astype(BF)
    weight_ref[...] = dot(spread, spread_ref[...])

    def potential_step(plane, carry):
        for copy in plane_in(plane):
            copy.wait()
        for yb in range(NG // 8):
            block = plane * (NG // 8) + yb
            cells = real_ref[block].astype(F32).reshape(8, 8, 256)
            values = pot_ref[block]
            values = jnp.concatenate([values, jnp.zeros((8, 64), F32)], axis=1)
            field_ref[block] = (cells * values[None]).reshape(64, 256)
        return carry

    lax.fori_loop(0, XD, potential_step, 0)
    projector_in.wait()
    own = (iota((8, 64), 1) // 8 == iota((8, 64), 0)).astype(F32)

    def slot(s, carry):
        rows = weight_ref[pl.ds(pl.multiple_of(s * 8, 8), 8), :]
        matrix = (rows[:, None, :] * own[None]).reshape(64, 64).astype(BF)
        block = slot_ref[s]
        field_ref[block, :, :NG] = field_ref[block, :, :NG] + dot(matrix, proj_ref[s])
        return carry

    lax.fori_loop(0, SD, slot, 0, unroll=8)

    def plane_step(plane, carry):
        start = plane * (NG // 8)
        parts = []
        for b in range(NBD):
            zero = field_ref[pl.ds(start, NG // 8), 16 * b : 16 * b + 8, :].reshape(NG, 256)
            one = field_ref[pl.ds(start, NG // 8), 16 * b + 8 : 16 * b + 16, :].reshape(NG, 256)
            cells = jnp.concatenate([zero, one], axis=1).astype(BF)
            parts.append(dot_nt(tz_ref[...], cells).astype(BF))
        both = dot(jnp.concatenate([part[:KB] for part in parts], axis=0), ty_ref[0])
        both = both + dot(jnp.concatenate([part[KB:] for part in parts], axis=0), ty_ref[1])
        for d in range(2):
            joined = join_bands(
                [both[KB * b : KB * b + KB, 128 * d : 128 * d + 128] for b in range(NBD)]
            )
            rows = pl.ds(d * XD + plane, ND, stride=DX)
            for h in range(HD):
                for v in range(3):
                    wide_ref[3 * h + v, rows, :] = joined[v][16 * h : 16 * h + 16]
        return carry

    lax.fori_loop(0, XD, plane_step, 0, unroll=PLANE_UNROLL)
    for t in range(TILES):
        out_ref[:, t * 128 : t * 128 + 128] = wide_ref[t].astype(BF)


def apply_part(tables, exchanged, own, kinds, mix, real_space, potential, projector, slot_block):
    spread = np.zeros((128, 64), np.float32)
    for p in range(8):
        spread[p * 8 : p * 8 + 8, p::8] = 1.0
    vmem, anywhere = pl.BlockSpec(memory_space=pltpu.VMEM), pl.BlockSpec(memory_space=pl.ANY)
    return pl.pallas_call(
        apply_kernel,
        in_specs=[pl.BlockSpec(memory_space=pltpu.SMEM)] + [vmem] * 7 + [anywhere] * 3,
        out_specs=vmem,
        out_shape=jax.ShapeDtypeStruct((ND * DX, LANES), BF),
        scratch_shapes=[
            pltpu.VMEM((NBLK, 64, 256), BF),
            pltpu.VMEM((NBLK, 8, NG), F32),
            pltpu.VMEM((SD, 64, NG), BF),
            pltpu.VMEM((NBLK, 64, 256), F32),
            pltpu.VMEM((TILES, ND * DX, 128), F32),
            pltpu.VMEM((SD * 8, 64), F32),
            pltpu.SemaphoreType.DMA((XD,)),
            pltpu.SemaphoreType.DMA((XD,)),
            pltpu.SemaphoreType.DMA,
        ],
        compiler_params=pltpu.CompilerParams(vmem_limit_bytes=59 * MIB),
        name="apply_part",
    )(
        slot_block, exchanged, own, kinds, mix, jnp.asarray(spread, BF),
        tables["cz"], tables["cy"], real_space, potential, projector,
    )


ROWS = HD * NBD
CHUNK = 2304
CHUNKS = KB * KB // CHUNK
HALF = KB * KB


def tail_kernel(
    kz_ref, table_ref, fold0_ref, fold1_ref, rows_ref, in_ref, wave_in_ref, all_in_ref,
    result_ref, out_ref,
    wave_ref, all_ref, spectrum_ref, wave_sem, all_sems,
):
    def chunk_in(c, i):
        columns = pl.ds(c * HALF + i * CHUNK, CHUNK)
        return pltpu.make_async_copy(
            all_in_ref.at[:, columns], all_ref.at[c, i], all_sems.at[c, i]
        )

    wave_in = pltpu.make_async_copy(wave_in_ref, wave_ref, wave_sem)
    wave_in.start()
    for i in range(CHUNKS):
        for c in range(2):
            chunk_in(c, i).start()
    for h in range(HD):
        spectrum = dot(table_ref[...], in_ref[:, h * GROUP : (h + 1) * GROUP])
        parts = split_bands(spectrum[:, :128], spectrum[:, 128:256], spectrum[:, 256:])
        for b in range(NBD):
            first = (h * NBD + b) * 2 * KB
            spectrum_ref[first : first + 2 * KB, :] = parts[b]
    wave_in.wait()

    kz = kz_ref[0] + iota((ROWS, 128), 0) // NBD - KB // 2
    kz = (kz * kz).astype(F32)
    entry = [iota((ROWS, 128), 1) + v * 128 for v in range(3)]
    row = [(e >= KB).astype(F32) + (e >= 2 * KB).astype(F32) + (e >= 3 * KB).astype(F32) for e in entry]
    ky = [entry[v].astype(F32) - KB * row[v] - KB // 2 for v in range(3)]
    fixed = [ky[v] * ky[v] + kz for v in range(3)]

    def flatten(group, carry):
        pieces = [
            spectrum_ref[pl.ds(group * 4 + v, ROWS, stride=2 * KB), :] for v in range(4)
        ]
        joined = join_bands(pieces)
        start = pl.multiple_of(group * GROUP, GROUP)
        first_kx = (lax.rem(group, KB // 4) * 4 - KB // 2).astype(F32)
        for v in range(3):
            columns = pl.ds(start + v * 128, 128)
            kx = row[v] + first_kx
            energy = (kx * kx + fixed[v]) * (2.0 / (KB * KB))
            value = joined[v] + energy * wave_ref[:, columns].astype(F32)
            result_ref[:, columns] = value.astype(BF)
        return carry

    lax.fori_loop(0, 2 * KB // 4, flatten, 0, unroll=4)

    total0, total1 = None, None
    for i in range(CHUNKS):
        low, high = slice(i * CHUNK, (i + 1) * CHUNK), slice(HALF + i * CHUNK, HALF + (i + 1) * CHUNK)
        right = [wave_ref[:, low], result_ref[:, low], wave_ref[:, high], result_ref[:, high]]
        right = jnp.concatenate([part.astype(F32) for part in right], axis=0).astype(BF)
        chunk_in(0, i).wait()
        term0 = dot_nt(right, all_ref[0, i])
        chunk_in(1, i).wait()
        term1 = dot_nt(right, all_ref[1, i])
        total0 = term0 if total0 is None else total0 + term0
        total1 = term1 if total1 is None else total1 + term1

    total0, total1 = total0.T, total1.T
    shape = total0.shape
    keep = iota(shape, 0) % ROWS // NBD == iota(shape, 1) % ROWS // NBD
    folded = jnp.dot(jnp.where(keep, total0, 0.0), fold0_ref[...], precision=HIGH) + jnp.dot(
        jnp.where(keep, total1, 0.0), fold1_ref[...], precision=HIGH
    )
    turned = jnp.dot(folded.T[:16], rows_ref[...], precision=HIGH)
    packed = jnp.where(iota((8, 128), 1) < 64, turned[:8], turned[8:])
    for k in range(ND):
        out_ref[k] = packed


def tail_part(table_x, first_kz, received, everything, wave):
    fold0 = np.zeros((2, 2, HD, NBD, 128), np.float32)
    fold1 = np.zeros((2, 2, HD, NBD, 128), np.float32)
    for k in range(2):
        for j in range(NBD):
            fold0[0, k, :, j, 4 * j + 2 * k] = 1.0
            fold0[1, k, :, j, 4 * j + 2 * k + 1] = 1.0
            fold1[1, k, :, j, 4 * j + 2 * k] = 1.0
            fold1[0, k, :, j, 4 * j + 2 * k + 1] = -1.0
    total = everything.shape[0]
    row = np.arange(total)
    band = row // ROWS * NBD + row % NBD
    rows = (band[:, None] == np.arange(128)[None, :] % 64).astype(np.float32)
    vmem, anywhere = pl.BlockSpec(memory_space=pltpu.VMEM), pl.BlockSpec(memory_space=pl.ANY)
    return pl.pallas_call(
        tail_kernel,
        in_specs=[pl.BlockSpec(memory_space=pltpu.SMEM)] + [vmem] * 5 + [anywhere] * 2,
        out_specs=[vmem, vmem],
        out_shape=[
            jax.ShapeDtypeStruct((ROWS, PLANE), BF),
            jax.ShapeDtypeStruct((ND, 8, 128), F32),
        ],
        scratch_shapes=[
            pltpu.VMEM((ROWS, PLANE), BF),
            pltpu.VMEM((2, CHUNKS, total, CHUNK), BF),
            pltpu.VMEM((ROWS * 2 * KB, 128), F32),
            pltpu.SemaphoreType.DMA,
            pltpu.SemaphoreType.DMA((2, CHUNKS)),
        ],
        compiler_params=pltpu.CompilerParams(vmem_limit_bytes=50 * MIB),
        name="tail_part",
    )(
        first_kz, table_x, jnp.asarray(fold0.reshape(-1, 128)), jnp.asarray(fold1.reshape(-1, 128)),
        jnp.asarray(rows), received, wave, everything,
    )


def exchange(array):
    return lax.all_to_all(array, "fft", split_axis=0, concat_axis=0, tiled=True)


def on_device(
    wave_coeffs,
    local_potential,
    projector,
    slot_block,
    slot_atom,
    atom_species,
    proj_count,
    projector_strength,
):
    tables = {name: jnp.asarray(value) for name, value in constants().items()}
    rows = wave_coeffs.transpose(1, 0, 2)
    wave = rows.reshape(HD, NBD, 2 * KB, KB)
    projector = projector.reshape(SD, NPROJ, 8, NG).transpose(0, 2, 1, 3).reshape(SD, 64, NG)
    potential = local_potential.reshape(NBLK, 8, NG)
    ids = jnp.concatenate(
        [(slot_atom // 32)[None], (slot_atom % 32)[None], jnp.zeros((14, SD), jnp.int32)]
    ).astype(BF)
    own_ids = jnp.broadcast_to(slot_atom.astype(F32)[:, None], (SD, 128))
    species = jnp.take(atom_species, slot_atom, axis=0)
    kinds = (species[:, None] == jnp.arange(256, dtype=jnp.int32)[None, :] // 64).astype(F32)
    symmetric = 0.5 * (projector_strength + jnp.swapaxes(projector_strength, 1, 2))
    active = (jnp.arange(NPROJ, dtype=jnp.int32)[None, :] < proj_count[:, None]).astype(F32)
    masked = symmetric * active[:, :, None] * active[:, None, :]
    mix = masked.transpose(2, 0, 1)[:, None, :, :, None] * jnp.eye(8, dtype=F32)[None, :, None, None]
    mix = jnp.pad(mix.reshape(64, 256), ((0, 64), (0, 0)))

    sent = x_transform(tables["a"], wave)
    sent, rows = lax.optimization_barrier((sent, rows))
    flat = rows.reshape(ROWS, PLANE)
    everything = lax.all_gather(flat, "band", axis=0, tiled=True)
    prepared = (ids, own_ids, kinds, mix, projector, potential)
    received = exchange(sent.reshape(ND, DX, LANES)).reshape(ND * DX, LANES)
    received, prepared = lax.optimization_barrier((received, prepared))
    ids, own_ids, kinds, mix, projector, potential = prepared
    terms, real_space = grid_part(tables, received, projector, slot_block, ids)
    exchanged = exchange(terms)
    sent = apply_part(
        tables, exchanged, own_ids, kinds, mix, real_space, potential, projector, slot_block
    )
    received = exchange(sent.reshape(ND, DX, LANES)).reshape(ND * DX, LANES)
    first_kz = (lax.axis_index("fft") * HD).astype(jnp.int32).reshape(1)
    result, partial = tail_part(tables["d"], first_kz, received, everything, flat)
    summed = exchange(partial).sum(axis=0) * (1.0 / (KB * KB * KB))
    subspace = summed.reshape(8, 2, 64).transpose(1, 0, 2).reshape(NBD, 4, 64)
    result_coeffs = result.reshape(HD, NBD, PLANE).transpose(1, 0, 2)
    return (result_coeffs, subspace)


def solution(mesh):
    return jax.shard_map(
        on_device,
        mesh=mesh,
        in_specs=(
            P("band", "fft", None),
            P("fft", None),
            P("fft", None, None),
            P("fft"),
            P("fft"),
            P(),
            P(),
            P(),
        ),
        out_specs=(P("band", "fft", None), P("band", None, None)),
        check_vma=False,
    )
```

```python
import math

import jax
import jax.numpy as jnp
import ml_dtypes
import numpy as np
from jax import lax
from jax.experimental import pallas as pl
from jax.experimental.pallas import tpu as pltpu
from jax.sharding import PartitionSpec as P

NG = 192
KB = 96
NPROJ = 8
NSPEC = 4
ND = 16
XD = NG // ND
HD = KB // ND
NBD = 4
SD = 128
NBLK = XD * NG // 8
DX = 2 * XD
LANES = HD * NBD * KB
TILES = LANES // 128
GROUP = NBD * KB
ROWS = HD * NBD
PLANE = 2 * KB * KB
BF = jnp.bfloat16
F32 = jnp.float32
HIGH = lax.Precision.HIGHEST
MIB = 1024 * 1024
PLANE_UNROLL = 6


def table(scaling, direction):
    phases = ((np.arange(KB) - KB // 2)[:, None] * np.arange(NG)[None, :]) % NG
    radians = phases.astype(np.float64) * (2.0 * math.pi / NG)
    cosine = np.cos(radians) / math.sqrt(scaling)
    sine = direction * np.sin(radians) / math.sqrt(scaling)
    full = np.stack([np.stack([cosine, sine]), np.stack([-sine, cosine])])
    return full.astype(np.float32).astype(ml_dtypes.bfloat16)


def pad_last(array, width):
    return np.pad(array, [(0, 0)] * (array.ndim - 1) + [(0, width - array.shape[-1])])


def constants():
    inverse = table(KB, 1.0)
    forward = table(NG, -1.0)
    out = {}
    inv_x = inverse.reshape(2, 2, KB, ND, XD)
    out["a"] = inv_x.transpose(3, 1, 4, 0, 2).reshape(ND * DX, 2 * KB)
    real_part = pad_last(inverse[0, 0].T, 128)
    imag_part = pad_last(inverse[0, 1].T, 128)
    out["by"] = np.concatenate([real_part, imag_part], axis=1)
    inv_z = inverse.reshape(2, 2, ND, HD, NG).transpose(0, 3, 2, 1, 4)
    out["bz"] = pad_last(inv_z, 256).reshape(2 * KB, 512)
    fwd_z = forward.reshape(2, 2, ND, HD, NG).transpose(1, 3, 2, 0, 4)
    out["cz"] = pad_last(fwd_z, 256).reshape(2 * KB, 512)
    out["cy"] = pad_last(forward.transpose(0, 3, 1, 2), 128).reshape(2, NG, 256)
    fwd_x = forward.reshape(2, 2, KB, ND, XD)
    out["d"] = fwd_x.transpose(1, 2, 3, 0, 4).reshape(2 * KB, ND * DX)
    return out


def dot(left, right):
    return jnp.dot(left, right, preferred_element_type=F32)


def dot_nt(left, right):
    return lax.dot_general(left, right, (((1,), (1,)), ((), ())), preferred_element_type=F32)


def iota(shape, axis):
    return lax.broadcasted_iota(jnp.int32, shape, axis)


def x_kernel(table_ref, wave_ref, out_ref):
    for h in range(HD):
        parts = [
            jnp.concatenate([wave_ref[h, b].astype(F32), jnp.zeros((2 * KB, 32), F32)], axis=1)
            for b in range(NBD)
        ]
        right = jnp.concatenate(join_bands(parts), axis=1).astype(BF)
        out_ref[:, h * GROUP : (h + 1) * GROUP] = dot(table_ref[...], right).astype(BF)


def x_transform(table_x, wave):
    return pl.pallas_call(
        x_kernel,
        out_shape=jax.ShapeDtypeStruct((ND * DX, LANES), BF),
        compiler_params=pltpu.CompilerParams(vmem_limit_bytes=24 * MIB),
        name="x_transform",
    )(table_x, wave)


def split_bands(first, second, third):
    lane = iota(first.shape, 1)
    one = pltpu.roll(jnp.where(lane >= 96, first, second), 32, 1)
    two = pltpu.roll(jnp.where(lane >= 64, second, third), 64, 1)
    return first, one, two, pltpu.roll(third, 96, 1)


def join_bands(parts):
    lane = iota(parts[0].shape, 1)
    one = pltpu.roll(parts[1], 96, 1)
    two = pltpu.roll(parts[2], 64, 1)
    three = pltpu.roll(parts[3], 32, 1)
    return (
        jnp.where(lane < 96, parts[0], one),
        jnp.where(lane < 64, one, two),
        jnp.where(lane < 32, two, three),
    )


def grid_kernel(
    slot_ref, ty_ref, tz_ref, fold_ref, ids_ref, in_ref, proj_in_ref,
    exch_ref, real_ref,
    proj_ref, wide_ref, space_ref, terms_ref, proj_sem, out_sems,
):
    def plane_out(plane):
        blocks = pl.ds(plane * (NG // 8), NG // 8)
        return pltpu.make_async_copy(space_ref.at[blocks], real_ref.at[blocks], out_sems.at[plane])

    projector_in = pltpu.make_async_copy(proj_in_ref, proj_ref, proj_sem)
    projector_in.start()
    for t in range(TILES):
        wide_ref[t] = in_ref[:, t * 128 : t * 128 + 128].astype(F32)

    def plane_step(plane, carry):
        pieces = []
        for d in range(2):
            rows = pl.ds(d * XD + plane, ND, stride=DX)
            columns = [
                jnp.concatenate([wide_ref[3 * h + v, rows, :] for h in range(HD)], axis=0)
                for v in range(3)
            ]
            pieces.append(split_bands(*columns))
        section = []
        for b in range(NBD):
            real_part, imag_part = pieces[0][b], pieces[1][b]
            right = jnp.concatenate(
                [
                    jnp.concatenate([real_part, -imag_part], axis=1),
                    jnp.concatenate([imag_part, real_part], axis=1),
                ],
                axis=0,
            ).astype(BF)
            section.append(dot_nt(ty_ref[...], right).astype(BF))
        whole = dot(jnp.concatenate(section, axis=0), tz_ref[...])
        for b in range(NBD):
            cells = whole[NG * b : NG * b + NG]
            both = jnp.concatenate(
                [cells[:, :256].reshape(NG // 8, 8, 256), cells[:, 256:].reshape(NG // 8, 8, 256)],
                axis=1,
            ).astype(BF)
            space_ref[pl.ds(plane * (NG // 8), NG // 8), 16 * b : 16 * b + 16, :] = both
        plane_out(plane).start()
        return carry

    lax.fori_loop(0, XD, plane_step, 0, unroll=PLANE_UNROLL)
    projector_in.wait()
    lane = iota((8, 64), 1) % 8

    def slot(s, carry):
        cells = space_ref[slot_ref[s]]
        product = dot_nt(proj_ref[s], cells[:, :NG]).reshape(8, 8, 64)
        total = jnp.where(lane == 0, product[0], 0.0)
        for y in range(1, 8):
            total = jnp.where(lane == y, product[y], total)
        terms_ref[pl.ds(pl.multiple_of(s * 8, 8), 8), :] = total
        return carry

    lax.fori_loop(0, SD, slot, 0, unroll=32)
    terms = terms_ref[...]
    high = terms.astype(BF)
    low = (terms - high.astype(F32)).astype(BF)
    folded = dot(high, fold_ref[...]) + dot(low, fold_ref[...])
    keep = iota(folded.shape, 0) % 8 == iota(folded.shape, 1) % 64 // 8
    folded = jnp.where(keep, folded, 0.0).astype(BF)
    sums = jnp.where(iota((SD, 1024), 1) // 8 == iota((SD, 1024), 0), 1.0, 0.0).astype(BF)
    ordered = dot(sums, folded)
    packed = jnp.where(iota((64, 128), 1) < 64, ordered[:64], ordered[64:]).astype(BF)
    for k in range(ND):
        exch_ref[k, 0:64, :] = packed
        exch_ref[k, 64:80, :] = ids_ref[...]
    for plane in range(XD):
        plane_out(plane).wait()


def grid_part(tables, received, projector, slot_block, ids):
    fold = np.zeros((64, 128), np.float32)
    for bc in range(8):
        for y in range(8):
            fold[bc * 8 + y, bc::8] = 1.0
    vmem, anywhere = pl.BlockSpec(memory_space=pltpu.VMEM), pl.BlockSpec(memory_space=pl.ANY)
    return pl.pallas_call(
        grid_kernel,
        in_specs=[pl.BlockSpec(memory_space=pltpu.SMEM)] + [vmem] * 5 + [anywhere],
        out_specs=[vmem, anywhere],
        out_shape=[
            jax.ShapeDtypeStruct((ND, 80, 128), BF),
            jax.ShapeDtypeStruct((NBLK, 64, 256), BF),
        ],
        scratch_shapes=[
            pltpu.VMEM((SD, 64, NG), BF),
            pltpu.VMEM((TILES, ND * DX, 128), F32),
            pltpu.VMEM((NBLK, 64, 256), BF),
            pltpu.VMEM((SD * 8, 64), F32),
            pltpu.SemaphoreType.DMA,
            pltpu.SemaphoreType.DMA((XD,)),
        ],
        compiler_params=pltpu.CompilerParams(vmem_limit_bytes=58 * MIB),
        name="grid_part",
    )(
        slot_block, tables["by"], tables["bz"], jnp.asarray(fold, BF), ids,
        received, projector,
    )


def apply_kernel(
    slot_ref, exch_in, ids_in, kinds_in, mix_in, spread_in, tz_in, ty_in,
    real_in_ref, pot_in_ref, proj_in_ref,
    out_ref,
    exch_ref, ids_ref, kinds_ref, mix_ref, spread_ref, tz_ref, ty_ref,
    real_ref, pot_ref, proj_ref, field_ref, wide_ref, weight_ref,
    small_sems, real_sems, pot_sems, proj_sem,
):
    def plane_in(plane):
        blocks = pl.ds(plane * (NG // 8), NG // 8)
        return (
            pltpu.make_async_copy(real_in_ref.at[blocks], real_ref.at[blocks], real_sems.at[plane]),
            pltpu.make_async_copy(pot_in_ref.at[blocks], pot_ref.at[blocks], pot_sems.at[plane]),
        )

    small_in_refs = (exch_in, ids_in, kinds_in, mix_in, spread_in, tz_in, ty_in)
    small_refs = (exch_ref, ids_ref, kinds_ref, mix_ref, spread_ref, tz_ref, ty_ref)
    small_in = [
        pltpu.make_async_copy(source, target, small_sems.at[i])
        for i, (source, target) in enumerate(zip(small_in_refs, small_refs))
    ]
    for copy in small_in:
        copy.start()
    for plane in range(XD):
        for copy in plane_in(plane):
            copy.start()
    projector_in = pltpu.make_async_copy(proj_in_ref, proj_ref, proj_sem)
    projector_in.start()

    for copy in small_in:
        copy.wait()
    own = ids_ref[...].astype(F32)
    own = jnp.broadcast_to(own[0:1] * 32.0 + own[1:2], (SD, 128)).T
    row, col = iota((128, 128), 0), iota((128, 128), 1)
    halves = (row < 64) == (col < 64)
    total = jnp.zeros((SD, 128), F32)
    for source in range(ND):
        ids = exch_ref[source, 64:80, :].astype(F32)
        atoms = ids[0:1] * 32.0 + ids[1:2]
        same = jnp.where(own == atoms, 1.0, 0.0).astype(BF)
        terms = exch_ref[source, 0:64, :].astype(F32)
        terms = jnp.where(halves, jnp.concatenate([terms, terms], axis=0), 0.0).astype(BF)
        total = total + dot(same, terms)
    total = total + pltpu.roll(total, 64, 1)
    mixed = jnp.dot(total, mix_ref[...], preferred_element_type=F32, precision=HIGH)
    mixed = mixed * kinds_ref[...]
    mixed = mixed[:, :128] + mixed[:, 128:]
    weighted = (mixed + pltpu.roll(mixed, 64, 1)).astype(BF)
    repeat = jnp.where(iota((1024, SD), 0) // 8 == iota((1024, SD), 1), 1.0, 0.0).astype(BF)
    spread = dot(repeat, weighted)
    keep = iota(spread.shape, 0) % 8 == iota(spread.shape, 1) % 8
    spread = jnp.where(keep, spread, 0.0).astype(BF)
    weight_ref[...] = dot(spread, spread_ref[...])

    def potential_step(plane, carry):
        for copy in plane_in(plane):
            copy.wait()
        for yb in range(NG // 8):
            block = plane * (NG // 8) + yb
            cells = real_ref[block].astype(F32).reshape(8, 8, 256)
            values = pot_ref[block]
            values = jnp.concatenate([values, jnp.zeros((8, 64), F32)], axis=1)
            field_ref[block] = (cells * values[None]).reshape(64, 256)
        return carry

    lax.fori_loop(0, XD, potential_step, 0)
    projector_in.wait()
    own = (iota((8, 64), 1) // 8 == iota((8, 64), 0)).astype(F32)

    def slot(s, carry):
        rows = weight_ref[pl.ds(pl.multiple_of(s * 8, 8), 8), :]
        matrix = (rows[:, None, :] * own[None]).reshape(64, 64).astype(BF)
        block = slot_ref[s]
        field_ref[block, :, :NG] = field_ref[block, :, :NG] + dot(matrix, proj_ref[s])
        return carry

    lax.fori_loop(0, SD, slot, 0, unroll=32)

    def plane_step(plane, carry):
        start = plane * (NG // 8)
        parts = []
        for b in range(NBD):
            zero = field_ref[pl.ds(start, NG // 8), 16 * b : 16 * b + 8, :].reshape(NG, 256)
            one = field_ref[pl.ds(start, NG // 8), 16 * b + 8 : 16 * b + 16, :].reshape(NG, 256)
            cells = jnp.concatenate([zero, one], axis=1).astype(BF)
            parts.append(dot_nt(tz_ref[...], cells).astype(BF))
        both = dot(jnp.concatenate([part[:KB] for part in parts], axis=0), ty_ref[0])
        both = both + dot(jnp.concatenate([part[KB:] for part in parts], axis=0), ty_ref[1])
        for d in range(2):
            joined = join_bands(
                [both[KB * b : KB * b + KB, 128 * d : 128 * d + 128] for b in range(NBD)]
            )
            rows = pl.ds(d * XD + plane, ND, stride=DX)
            for h in range(HD):
                for v in range(3):
                    wide_ref[3 * h + v, rows, :] = joined[v][16 * h : 16 * h + 16]
        return carry

    lax.fori_loop(0, XD, plane_step, 0, unroll=PLANE_UNROLL)
    for t in range(TILES):
        out_ref[:, t * 128 : t * 128 + 128] = wide_ref[t].astype(BF)


def apply_part(tables, exchanged, ids, kinds, mix, real_space, potential, projector, slot_block):
    spread = np.zeros((128, 64), np.float32)
    for p in range(8):
        spread[p * 8 : p * 8 + 8, p::8] = 1.0
    vmem, anywhere = pl.BlockSpec(memory_space=pltpu.VMEM), pl.BlockSpec(memory_space=pl.ANY)
    return pl.pallas_call(
        apply_kernel,
        in_specs=[pl.BlockSpec(memory_space=pltpu.SMEM)] + [anywhere] * 10,
        out_specs=vmem,
        out_shape=jax.ShapeDtypeStruct((ND * DX, LANES), BF),
        scratch_shapes=[
            pltpu.VMEM((ND, 80, 128), BF),
            pltpu.VMEM((16, 128), BF),
            pltpu.VMEM((SD, 256), F32),
            pltpu.VMEM((128, 256), F32),
            pltpu.VMEM((128, 64), BF),
            pltpu.VMEM((2 * KB, 512), BF),
            pltpu.VMEM((2, NG, 256), BF),
            pltpu.VMEM((NBLK, 64, 256), BF),
            pltpu.VMEM((NBLK, 8, NG), F32),
            pltpu.VMEM((SD, 64, NG), BF),
            pltpu.VMEM((NBLK, 64, 256), F32),
            pltpu.VMEM((TILES, ND * DX, 128), F32),
            pltpu.VMEM((SD * 8, 64), F32),
            pltpu.SemaphoreType.DMA((7,)),
            pltpu.SemaphoreType.DMA((XD,)),
            pltpu.SemaphoreType.DMA((XD,)),
            pltpu.SemaphoreType.DMA,
        ],
        compiler_params=pltpu.CompilerParams(vmem_limit_bytes=59 * MIB),
        name="apply_part",
    )(
        slot_block, exchanged, ids, kinds, mix, jnp.asarray(spread, BF),
        tables["cz"], tables["cy"], real_space, potential, projector,
    )


CHUNK = 2304
CHUNKS = KB * KB // CHUNK
HALF = KB * KB


def tail_kernel(
    kz_ref, table_ref, in_ref, wave_in_ref, all_in_ref,
    result_ref, out_ref,
    wave_ref, all_ref, spectrum_ref, wave_sem, all_sems,
):
    def chunk_in(c, i):
        columns = pl.ds(c * HALF + i * CHUNK, CHUNK)
        return pltpu.make_async_copy(
            all_in_ref.at[:, columns], all_ref.at[c, i], all_sems.at[c, i]
        )

    wave_in = pltpu.make_async_copy(wave_in_ref, wave_ref, wave_sem)
    wave_in.start()
    for i in range(CHUNKS):
        for c in range(2):
            chunk_in(c, i).start()
    for h in range(HD):
        spectrum = dot(table_ref[...], in_ref[:, h * GROUP : (h + 1) * GROUP])
        parts = split_bands(spectrum[:, :128], spectrum[:, 128:256], spectrum[:, 256:])
        for b in range(NBD):
            first = (h * NBD + b) * 2 * KB
            spectrum_ref[first : first + 2 * KB, :] = parts[b]
    wave_in.wait()

    kz = kz_ref[0] + iota((ROWS, 128), 0) // NBD - KB // 2
    kz = (kz * kz).astype(F32)
    entry = [iota((ROWS, 128), 1) + v * 128 for v in range(3)]
    row = [(e >= KB).astype(F32) + (e >= 2 * KB).astype(F32) + (e >= 3 * KB).astype(F32) for e in entry]
    ky = [entry[v].astype(F32) - KB * row[v] - KB // 2 for v in range(3)]
    fixed = [ky[v] * ky[v] + kz for v in range(3)]

    def flatten(group, carry):
        pieces = [
            spectrum_ref[pl.ds(group * 4 + v, ROWS, stride=2 * KB), :] for v in range(4)
        ]
        joined = join_bands(pieces)
        start = pl.multiple_of(group * GROUP, GROUP)
        first_kx = (lax.rem(group, KB // 4) * 4 - KB // 2).astype(F32)
        for v in range(3):
            columns = pl.ds(start + v * 128, 128)
            kx = row[v] + first_kx
            energy = (kx * kx + fixed[v]) * (2.0 / (KB * KB))
            value = joined[v] + energy * wave_ref[:, columns].astype(F32)
            result_ref[:, columns] = value.astype(BF)
        return carry

    lax.fori_loop(0, 2 * KB // 4, flatten, 0, unroll=8)

    total0, total1 = None, None
    for i in range(CHUNKS):
        low, high = slice(i * CHUNK, (i + 1) * CHUNK), slice(HALF + i * CHUNK, HALF + (i + 1) * CHUNK)
        right = [wave_ref[:, low], result_ref[:, low], wave_ref[:, high], result_ref[:, high]]
        right = jnp.concatenate([part.astype(F32) for part in right], axis=0).astype(BF)
        chunk_in(0, i).wait()
        term0 = dot_nt(right, all_ref[0, i])
        chunk_in(1, i).wait()
        term1 = dot_nt(right, all_ref[1, i])
        total0 = term0 if total0 is None else total0 + term0
        total1 = term1 if total1 is None else total1 + term1

    total0, total1 = total0.T, total1.T
    shape = total0.shape
    keep = iota(shape, 0) % ROWS // NBD == iota(shape, 1) % ROWS // NBD
    row, col = iota((4 * ROWS, 128), 0), iota((4 * ROWS, 128), 1)
    place = row % NBD * 4 + row // ROWS % 2 * 2
    d = row // (2 * ROWS)
    fold0 = jnp.where(col == place + d, 1.0, 0.0)
    fold1 = jnp.where(col == place + 1 - d, 2.0 * d.astype(F32) - 1.0, 0.0)
    row, col = iota((shape[0], 128), 0), iota((shape[0], 128), 1)
    bands = jnp.where(row // ROWS * NBD + row % NBD == col % 64, 1.0, 0.0)
    folded = jnp.dot(jnp.where(keep, total0, 0.0), fold0, precision=HIGH) + jnp.dot(
        jnp.where(keep, total1, 0.0), fold1, precision=HIGH
    )
    turned = jnp.dot(folded.T[:16], bands, precision=HIGH)
    packed = jnp.where(iota((8, 128), 1) < 64, turned[:8], turned[8:])
    for k in range(ND):
        out_ref[k] = packed


def tail_part(table_x, first_kz, received, everything, wave):
    total = everything.shape[0]
    vmem, anywhere = pl.BlockSpec(memory_space=pltpu.VMEM), pl.BlockSpec(memory_space=pl.ANY)
    return pl.pallas_call(
        tail_kernel,
        in_specs=[pl.BlockSpec(memory_space=pltpu.SMEM)] + [vmem] * 2 + [anywhere] * 2,
        out_specs=[vmem, vmem],
        out_shape=[
            jax.ShapeDtypeStruct((ROWS, PLANE), BF),
            jax.ShapeDtypeStruct((ND, 8, 128), F32),
        ],
        scratch_shapes=[
            pltpu.VMEM((ROWS, PLANE), BF),
            pltpu.VMEM((2, CHUNKS, total, CHUNK), BF),
            pltpu.VMEM((ROWS * 2 * KB, 128), F32),
            pltpu.SemaphoreType.DMA,
            pltpu.SemaphoreType.DMA((2, CHUNKS)),
        ],
        compiler_params=pltpu.CompilerParams(vmem_limit_bytes=50 * MIB),
        name="tail_part",
    )(
        first_kz, table_x, received, wave, everything,
    )


def exchange(array):
    return lax.all_to_all(array, "fft", split_axis=0, concat_axis=0, tiled=True)


def on_device(
    wave_coeffs,
    local_potential,
    projector,
    slot_block,
    slot_atom,
    atom_species,
    proj_count,
    projector_strength,
):
    tables = {name: jnp.asarray(value) for name, value in constants().items()}
    rows = wave_coeffs.transpose(1, 0, 2)
    wave = rows.reshape(HD, NBD, 2 * KB, KB)

    projector = projector.reshape(SD, NPROJ, 8, NG).transpose(0, 2, 1, 3).reshape(SD, 64, NG)
    potential = local_potential.reshape(NBLK, 8, NG)
    ids = jnp.concatenate(
        [(slot_atom // 32)[None], (slot_atom % 32)[None], jnp.zeros((14, SD), jnp.int32)]
    ).astype(BF)
    species = jnp.take(atom_species, slot_atom, axis=0)
    kinds = (species[:, None] == jnp.arange(256, dtype=jnp.int32)[None, :] // 64).astype(F32)
    symmetric = 0.5 * (projector_strength + jnp.swapaxes(projector_strength, 1, 2))
    active = (jnp.arange(NPROJ, dtype=jnp.int32)[None, :] < proj_count[:, None]).astype(F32)
    masked = symmetric * active[:, :, None] * active[:, None, :]
    mix = masked.transpose(2, 0, 1)[:, None, :, :, None] * jnp.eye(8, dtype=F32)[None, :, None, None]
    mix = jnp.pad(mix.reshape(64, 256), ((0, 64), (0, 0)))

    sent = x_transform(tables["a"], wave)
    sent, rows = lax.optimization_barrier((sent, rows))
    flat = rows.reshape(ROWS, PLANE)
    everything = lax.all_gather(flat, "band", axis=0, tiled=True)
    prepared = (ids, kinds, mix, projector, potential)
    received = exchange(sent.reshape(ND, DX, LANES)).reshape(ND * DX, LANES)
    received, prepared = lax.optimization_barrier((received, prepared))
    ids, kinds, mix, projector, potential = prepared
    terms, real_space = grid_part(tables, received, projector, slot_block, ids)
    exchanged = exchange(terms)
    sent = apply_part(
        tables, exchanged, ids, kinds, mix, real_space, potential, projector, slot_block
    )
    received = exchange(sent.reshape(ND, DX, LANES)).reshape(ND * DX, LANES)
    first_kz = (lax.axis_index("fft") * HD).astype(jnp.int32).reshape(1)
    result, partial = tail_part(tables["d"], first_kz, received, everything, flat)
    summed = exchange(partial).sum(axis=0) * (1.0 / (KB * KB * KB))
    subspace = summed.reshape(8, 2, 64).transpose(1, 0, 2).reshape(NBD, 4, 64)
    result_coeffs = result.reshape(HD, NBD, PLANE).transpose(1, 0, 2)
    return (result_coeffs, subspace)


def solution(mesh):
    return jax.shard_map(
        on_device,
        mesh=mesh,
        in_specs=(
            P("band", "fft", None),
            P("fft", None),
            P("fft", None, None),
            P("fft"),
            P("fft"),
            P(),
            P(),
            P(),
        ),
        out_specs=(P("band", "fft", None), P("band", None, None)),
        check_vma=False,
    )
```

```python
import math

import jax
import jax.numpy as jnp
import ml_dtypes
import numpy as np
from jax import lax
from jax.experimental import pallas as pl
from jax.experimental.pallas import tpu as pltpu
from jax.sharding import PartitionSpec as P

NG = 192
KB = 96
NPROJ = 8
NSPEC = 4
ND = 16
XD = NG // ND
HD = KB // ND
NBD = 4
SD = 128
NBLK = XD * NG // 8
DX = 2 * XD
LANES = HD * NBD * KB
TILES = LANES // 128
GROUP = NBD * KB
ROWS = HD * NBD
PLANE = 2 * KB * KB
BF = jnp.bfloat16
F32 = jnp.float32
HIGH = lax.Precision.HIGHEST
MIB = 1024 * 1024
PLANE_UNROLL = 6


def table(scaling, direction):
    phases = ((np.arange(KB) - KB // 2)[:, None] * np.arange(NG)[None, :]) % NG
    radians = phases.astype(np.float64) * (2.0 * math.pi / NG)
    cosine = np.cos(radians) / math.sqrt(scaling)
    sine = direction * np.sin(radians) / math.sqrt(scaling)
    full = np.stack([np.stack([cosine, sine]), np.stack([-sine, cosine])])
    return full.astype(np.float32).astype(ml_dtypes.bfloat16)


def pad_last(array, width):
    return np.pad(array, [(0, 0)] * (array.ndim - 1) + [(0, width - array.shape[-1])])


def constants():
    inverse = table(KB, 1.0)
    forward = table(NG, -1.0)
    out = {}
    inv_x = inverse.reshape(2, 2, KB, ND, XD)
    out["a"] = inv_x.transpose(3, 1, 4, 0, 2).reshape(ND * DX, 2 * KB)
    real_part = pad_last(inverse[0, 0].T, 128)
    imag_part = pad_last(inverse[0, 1].T, 128)
    out["by"] = np.concatenate([real_part, imag_part], axis=1)
    inv_z = inverse.reshape(2, 2, ND, HD, NG).transpose(0, 3, 2, 1, 4)
    out["bz"] = pad_last(inv_z, 256).reshape(2 * KB, 512)
    fwd_z = forward.reshape(2, 2, ND, HD, NG).transpose(1, 3, 2, 0, 4)
    out["cz"] = pad_last(fwd_z, 256).reshape(2 * KB, 512)
    out["cy"] = pad_last(forward.transpose(0, 3, 1, 2), 128).reshape(2, NG, 256)
    fwd_x = forward.reshape(2, 2, KB, ND, XD)
    out["d"] = fwd_x.transpose(1, 2, 3, 0, 4).reshape(2 * KB, ND * DX)
    return out


def dot(left, right):
    return jnp.dot(left, right, preferred_element_type=F32)


def dot_nt(left, right):
    return lax.dot_general(left, right, (((1,), (1,)), ((), ())), preferred_element_type=F32)


def iota(shape, axis):
    return lax.broadcasted_iota(jnp.int32, shape, axis)


def x_kernel(table_ref, wave_ref, out_ref):
    for h in range(HD):
        parts = [
            jnp.concatenate([wave_ref[h, b].astype(F32), jnp.zeros((2 * KB, 32), F32)], axis=1)
            for b in range(NBD)
        ]
        right = jnp.concatenate(join_bands(parts), axis=1).astype(BF)
        out_ref[:, h * GROUP : (h + 1) * GROUP] = dot(table_ref[...], right).astype(BF)


def x_transform(table_x, wave):
    return pl.pallas_call(
        x_kernel,
        out_shape=jax.ShapeDtypeStruct((ND * DX, LANES), BF),
        compiler_params=pltpu.CompilerParams(vmem_limit_bytes=24 * MIB),
        name="x_transform",
    )(table_x, wave)


def split_bands(first, second, third):
    lane = iota(first.shape, 1)
    one = pltpu.roll(jnp.where(lane >= 96, first, second), 32, 1)
    two = pltpu.roll(jnp.where(lane >= 64, second, third), 64, 1)
    return first, one, two, pltpu.roll(third, 96, 1)


def join_bands(parts):
    lane = iota(parts[0].shape, 1)
    one = pltpu.roll(parts[1], 96, 1)
    two = pltpu.roll(parts[2], 64, 1)
    three = pltpu.roll(parts[3], 32, 1)
    return (
        jnp.where(lane < 96, parts[0], one),
        jnp.where(lane < 64, one, two),
        jnp.where(lane < 32, two, three),
    )


def grid_kernel(
    slot_ref, ty_ref, tz_ref, fold_ref, ids_ref, in_ref, proj_in_ref,
    exch_ref, real_ref,
    proj_ref, wide_ref, space_ref, terms_ref, proj_sem, out_sems,
):
    def plane_out(plane):
        blocks = pl.ds(plane * (NG // 8), NG // 8)
        return pltpu.make_async_copy(space_ref.at[blocks], real_ref.at[blocks], out_sems.at[plane])

    projector_in = pltpu.make_async_copy(proj_in_ref, proj_ref, proj_sem)
    projector_in.start()
    for t in range(TILES):
        wide_ref[t] = in_ref[:, t * 128 : t * 128 + 128].astype(F32)

    def plane_step(plane, carry):
        pieces = []
        for d in range(2):
            rows = pl.ds(d * XD + plane, ND, stride=DX)
            columns = [
                jnp.concatenate([wide_ref[3 * h + v, rows, :] for h in range(HD)], axis=0)
                for v in range(3)
            ]
            pieces.append(split_bands(*columns))
        section = []
        for b in range(NBD):
            real_part, imag_part = pieces[0][b], pieces[1][b]
            right = jnp.concatenate(
                [
                    jnp.concatenate([real_part, -imag_part], axis=1),
                    jnp.concatenate([imag_part, real_part], axis=1),
                ],
                axis=0,
            ).astype(BF)
            section.append(dot_nt(ty_ref[...], right).astype(BF))
        whole = dot(jnp.concatenate(section, axis=0), tz_ref[...])
        for b in range(NBD):
            cells = whole[NG * b : NG * b + NG]
            both = jnp.concatenate(
                [cells[:, :256].reshape(NG // 8, 8, 256), cells[:, 256:].reshape(NG // 8, 8, 256)],
                axis=1,
            ).astype(BF)
            space_ref[pl.ds(plane * (NG // 8), NG // 8), 16 * b : 16 * b + 16, :] = both
        plane_out(plane).start()
        return carry

    lax.fori_loop(0, XD, plane_step, 0, unroll=PLANE_UNROLL)
    projector_in.wait()
    lane = iota((8, 64), 1) % 8

    def slot(s, carry):
        cells = space_ref[slot_ref[s]]
        product = dot_nt(proj_ref[s], cells[:, :NG]).reshape(8, 8, 64)
        total = jnp.where(lane == 0, product[0], 0.0)
        for y in range(1, 8):
            total = jnp.where(lane == y, product[y], total)
        terms_ref[pl.ds(pl.multiple_of(s * 8, 8), 8), :] = total
        return carry

    lax.fori_loop(0, SD, slot, 0, unroll=32)
    terms = terms_ref[...]
    high = terms.astype(BF)
    low = (terms - high.astype(F32)).astype(BF)
    folded = dot(high, fold_ref[...]) + dot(low, fold_ref[...])
    keep = iota(folded.shape, 0) % 8 == iota(folded.shape, 1) % 64 // 8
    folded = jnp.where(keep, folded, 0.0).astype(BF)
    sums = jnp.where(iota((SD, 1024), 1) // 8 == iota((SD, 1024), 0), 1.0, 0.0).astype(BF)
    ordered = dot(sums, folded)
    packed = jnp.where(iota((64, 128), 1) < 64, ordered[:64], ordered[64:]).astype(BF)
    for k in range(ND):
        exch_ref[k, 0:64, :] = packed
        exch_ref[k, 64:80, :] = ids_ref[...]
    for plane in range(XD):
        plane_out(plane).wait()


def grid_part(tables, received, projector, slot_block, ids):
    fold = np.zeros((64, 128), np.float32)
    for bc in range(8):
        for y in range(8):
            fold[bc * 8 + y, bc::8] = 1.0
    vmem, anywhere = pl.BlockSpec(memory_space=pltpu.VMEM), pl.BlockSpec(memory_space=pl.ANY)
    return pl.pallas_call(
        grid_kernel,
        in_specs=[pl.BlockSpec(memory_space=pltpu.SMEM)] + [vmem] * 5 + [anywhere],
        out_specs=[vmem, anywhere],
        out_shape=[
            jax.ShapeDtypeStruct((ND, 80, 128), BF),
            jax.ShapeDtypeStruct((NBLK, 64, 256), BF),
        ],
        scratch_shapes=[
            pltpu.VMEM((SD, 64, NG), BF),
            pltpu.VMEM((TILES, ND * DX, 128), F32),
            pltpu.VMEM((NBLK, 64, 256), BF),
            pltpu.VMEM((SD * 8, 64), F32),
            pltpu.SemaphoreType.DMA,
            pltpu.SemaphoreType.DMA((XD,)),
        ],
        compiler_params=pltpu.CompilerParams(vmem_limit_bytes=58 * MIB),
        name="grid_part",
    )(
        slot_block, tables["by"], tables["bz"], jnp.asarray(fold, BF), ids,
        received, projector,
    )


def apply_kernel(
    slot_ref, exch_in, ids_in, kinds_in, mix_in, spread_in, tz_in, ty_in,
    real_in_ref, pot_in_ref, proj_in_ref,
    out_ref,
    exch_ref, ids_ref, kinds_ref, mix_ref, spread_ref, tz_ref, ty_ref,
    real_ref, pot_ref, proj_ref, field_ref, wide_ref, weight_ref, sent_ref,
    small_sems, real_sems, pot_sems, proj_sem, out_sems,
):
    def plane_in(plane):
        blocks = pl.ds(plane * (NG // 8), NG // 8)
        return (
            pltpu.make_async_copy(real_in_ref.at[blocks], real_ref.at[blocks], real_sems.at[plane]),
            pltpu.make_async_copy(pot_in_ref.at[blocks], pot_ref.at[blocks], pot_sems.at[plane]),
        )

    small_in_refs = (exch_in, ids_in, kinds_in, mix_in, spread_in, tz_in, ty_in)
    small_refs = (exch_ref, ids_ref, kinds_ref, mix_ref, spread_ref, tz_ref, ty_ref)
    small_in = [
        pltpu.make_async_copy(source, target, small_sems.at[i])
        for i, (source, target) in enumerate(zip(small_in_refs, small_refs))
    ]
    for copy in small_in:
        copy.start()
    for plane in range(XD):
        for copy in plane_in(plane):
            copy.start()
    projector_in = pltpu.make_async_copy(proj_in_ref, proj_ref, proj_sem)
    projector_in.start()

    for copy in small_in:
        copy.wait()
    own = ids_ref[...].astype(F32)
    own = jnp.broadcast_to(own[0:1] * 32.0 + own[1:2], (SD, 128)).T
    row, col = iota((128, 128), 0), iota((128, 128), 1)
    halves = (row < 64) == (col < 64)
    total = jnp.zeros((SD, 128), F32)
    for source in range(ND):
        ids = exch_ref[source, 64:80, :].astype(F32)
        atoms = ids[0:1] * 32.0 + ids[1:2]
        same = jnp.where(own == atoms, 1.0, 0.0).astype(BF)
        terms = exch_ref[source, 0:64, :].astype(F32)
        terms = jnp.where(halves, jnp.concatenate([terms, terms], axis=0), 0.0).astype(BF)
        total = total + dot(same, terms)
    total = total + pltpu.roll(total, 64, 1)
    mixed = jnp.dot(total, mix_ref[...], preferred_element_type=F32, precision=HIGH)
    mixed = mixed * kinds_ref[...]
    mixed = mixed[:, :128] + mixed[:, 128:]
    weighted = (mixed + pltpu.roll(mixed, 64, 1)).astype(BF)
    repeat = jnp.where(iota((1024, SD), 0) // 8 == iota((1024, SD), 1), 1.0, 0.0).astype(BF)
    spread = dot(repeat, weighted)
    keep = iota(spread.shape, 0) % 8 == iota(spread.shape, 1) % 8
    spread = jnp.where(keep, spread, 0.0).astype(BF)
    weight_ref[...] = dot(spread, spread_ref[...])

    def potential_step(plane, carry):
        for copy in plane_in(plane):
            copy.wait()
        for yb in range(NG // 8):
            block = plane * (NG // 8) + yb
            cells = real_ref[block].astype(F32).reshape(8, 8, 256)
            values = pot_ref[block]
            values = jnp.concatenate([values, jnp.zeros((8, 64), F32)], axis=1)
            field_ref[block] = (cells * values[None]).reshape(64, 256)
        return carry

    lax.fori_loop(0, XD, potential_step, 0)
    projector_in.wait()
    own = (iota((8, 64), 1) // 8 == iota((8, 64), 0)).astype(F32)

    def slot(s, carry):
        rows = weight_ref[pl.ds(pl.multiple_of(s * 8, 8), 8), :]
        matrix = (rows[:, None, :] * own[None]).reshape(64, 64).astype(BF)
        block = slot_ref[s]
        field_ref[block, :, :NG] = field_ref[block, :, :NG] + dot(matrix, proj_ref[s])
        return carry

    lax.fori_loop(0, SD, slot, 0, unroll=64)

    def plane_step(plane, carry):
        start = plane * (NG // 8)
        parts = []
        for b in range(NBD):
            zero = field_ref[pl.ds(start, NG // 8), 16 * b : 16 * b + 8, :].reshape(NG, 256)
            one = field_ref[pl.ds(start, NG // 8), 16 * b + 8 : 16 * b + 16, :].reshape(NG, 256)
            cells = jnp.concatenate([zero, one], axis=1).astype(BF)
            parts.append(dot_nt(tz_ref[...], cells).astype(BF))
        both = dot(jnp.concatenate([part[:KB] for part in parts], axis=0), ty_ref[0])
        both = both + dot(jnp.concatenate([part[KB:] for part in parts], axis=0), ty_ref[1])
        for d in range(2):
            joined = join_bands(
                [both[KB * b : KB * b + KB, 128 * d : 128 * d + 128] for b in range(NBD)]
            )
            rows = pl.ds(d * XD + plane, ND, stride=DX)
            for h in range(HD):
                for v in range(3):
                    wide_ref[3 * h + v, rows, :] = joined[v][16 * h : 16 * h + 16]
        return carry

    lax.fori_loop(0, XD, plane_step, 0, unroll=XD)
    def columns_out(h):
        columns = pl.ds(h * GROUP, GROUP)
        return pltpu.make_async_copy(sent_ref.at[:, columns], out_ref.at[:, columns], out_sems.at[h])

    for h in range(HD):
        for t in range(3 * h, 3 * h + 3):
            sent_ref[:, t * 128 : t * 128 + 128] = wide_ref[t].astype(BF)
        columns_out(h).start()
    for h in range(HD):
        columns_out(h).wait()


def apply_part(tables, exchanged, ids, kinds, mix, real_space, potential, projector, slot_block):
    spread = np.zeros((128, 64), np.float32)
    for p in range(8):
        spread[p * 8 : p * 8 + 8, p::8] = 1.0
    anywhere = pl.BlockSpec(memory_space=pl.ANY)
    return pl.pallas_call(
        apply_kernel,
        in_specs=[pl.BlockSpec(memory_space=pltpu.SMEM)] + [anywhere] * 10,
        out_specs=anywhere,
        out_shape=jax.ShapeDtypeStruct((ND * DX, LANES), BF),
        scratch_shapes=[
            pltpu.VMEM((ND, 80, 128), BF),
            pltpu.VMEM((16, 128), BF),
            pltpu.VMEM((SD, 256), F32),
            pltpu.VMEM((128, 256), F32),
            pltpu.VMEM((128, 64), BF),
            pltpu.VMEM((2 * KB, 512), BF),
            pltpu.VMEM((2, NG, 256), BF),
            pltpu.VMEM((NBLK, 64, 256), BF),
            pltpu.VMEM((NBLK, 8, NG), F32),
            pltpu.VMEM((SD, 64, NG), BF),
            pltpu.VMEM((NBLK, 64, 256), F32),
            pltpu.VMEM((TILES, ND * DX, 128), F32),
            pltpu.VMEM((SD * 8, 64), F32),
            pltpu.VMEM((ND * DX, LANES), BF),
            pltpu.SemaphoreType.DMA((7,)),
            pltpu.SemaphoreType.DMA((XD,)),
            pltpu.SemaphoreType.DMA((XD,)),
            pltpu.SemaphoreType.DMA,
            pltpu.SemaphoreType.DMA((HD,)),
        ],
        compiler_params=pltpu.CompilerParams(vmem_limit_bytes=59 * MIB),
        name="apply_part",
    )(
        slot_block, exchanged, ids, kinds, mix, jnp.asarray(spread, BF),
        tables["cz"], tables["cy"], real_space, potential, projector,
    )


CHUNK = 2304
CHUNKS = KB * KB // CHUNK
HALF = KB * KB


def tail_kernel(
    kz_ref, table_ref, in_ref, wave_in_ref, all_in_ref,
    result_ref, out_ref,
    wave_ref, all_ref, spectrum_ref, wave_sem, all_sems,
):
    def chunk_in(c, i):
        columns = pl.ds(c * HALF + i * CHUNK, CHUNK)
        return pltpu.make_async_copy(
            all_in_ref.at[:, columns], all_ref.at[c, i], all_sems.at[c, i]
        )

    wave_in = pltpu.make_async_copy(wave_in_ref, wave_ref, wave_sem)
    wave_in.start()
    for i in range(CHUNKS):
        for c in range(2):
            chunk_in(c, i).start()
    for h in range(HD):
        spectrum = dot(table_ref[...], in_ref[:, h * GROUP : (h + 1) * GROUP])
        parts = split_bands(spectrum[:, :128], spectrum[:, 128:256], spectrum[:, 256:])
        for b in range(NBD):
            first = (h * NBD + b) * 2 * KB
            spectrum_ref[first : first + 2 * KB, :] = parts[b]
    wave_in.wait()

    kz = kz_ref[0] + iota((ROWS, 128), 0) // NBD - KB // 2
    kz = (kz * kz).astype(F32)
    entry = [iota((ROWS, 128), 1) + v * 128 for v in range(3)]
    row = [(e >= KB).astype(F32) + (e >= 2 * KB).astype(F32) + (e >= 3 * KB).astype(F32) for e in entry]
    ky = [entry[v].astype(F32) - KB * row[v] - KB // 2 for v in range(3)]
    fixed = [ky[v] * ky[v] + kz for v in range(3)]

    def flatten(group, carry):
        pieces = [
            spectrum_ref[pl.ds(group * 4 + v, ROWS, stride=2 * KB), :] for v in range(4)
        ]
        joined = join_bands(pieces)
        start = pl.multiple_of(group * GROUP, GROUP)
        first_kx = (lax.rem(group, KB // 4) * 4 - KB // 2).astype(F32)
        for v in range(3):
            columns = pl.ds(start + v * 128, 128)
            kx = row[v] + first_kx
            energy = (kx * kx + fixed[v]) * (2.0 / (KB * KB))
            value = joined[v] + energy * wave_ref[:, columns].astype(F32)
            result_ref[:, columns] = value.astype(BF)
        return carry

    lax.fori_loop(0, 2 * KB // 4, flatten, 0, unroll=8)

    total0, total1 = None, None
    for i in range(CHUNKS):
        low, high = slice(i * CHUNK, (i + 1) * CHUNK), slice(HALF + i * CHUNK, HALF + (i + 1) * CHUNK)
        right = [wave_ref[:, low], result_ref[:, low], wave_ref[:, high], result_ref[:, high]]
        right = jnp.concatenate([part.astype(F32) for part in right], axis=0).astype(BF)
        chunk_in(0, i).wait()
        term0 = dot_nt(right, all_ref[0, i])
        chunk_in(1, i).wait()
        term1 = dot_nt(right, all_ref[1, i])
        total0 = term0 if total0 is None else total0 + term0
        total1 = term1 if total1 is None else total1 + term1

    total0, total1 = total0.T, total1.T
    shape = total0.shape
    keep = iota(shape, 0) % ROWS // NBD == iota(shape, 1) % ROWS // NBD
    row, col = iota((4 * ROWS, 128), 0), iota((4 * ROWS, 128), 1)
    place = row % NBD * 4 + row // ROWS % 2 * 2
    d = row // (2 * ROWS)
    fold0 = jnp.where(col == place + d, 1.0, 0.0)
    fold1 = jnp.where(col == place + 1 - d, 2.0 * d.astype(F32) - 1.0, 0.0)
    row, col = iota((shape[0], 128), 0), iota((shape[0], 128), 1)
    bands = jnp.where(row // ROWS * NBD + row % NBD == col % 64, 1.0, 0.0)
    folded = jnp.dot(jnp.where(keep, total0, 0.0), fold0, precision=HIGH) + jnp.dot(
        jnp.where(keep, total1, 0.0), fold1, precision=HIGH
    )
    turned = jnp.dot(folded.T[:16], bands, precision=HIGH)
    packed = jnp.where(iota((8, 128), 1) < 64, turned[:8], turned[8:])
    for k in range(ND):
        out_ref[k] = packed


def tail_part(table_x, first_kz, received, everything, wave):
    total = everything.shape[0]
    vmem, anywhere = pl.BlockSpec(memory_space=pltpu.VMEM), pl.BlockSpec(memory_space=pl.ANY)
    return pl.pallas_call(
        tail_kernel,
        in_specs=[pl.BlockSpec(memory_space=pltpu.SMEM)] + [vmem] * 2 + [anywhere] * 2,
        out_specs=[vmem, vmem],
        out_shape=[
            jax.ShapeDtypeStruct((ROWS, PLANE), BF),
            jax.ShapeDtypeStruct((ND, 8, 128), F32),
        ],
        scratch_shapes=[
            pltpu.VMEM((ROWS, PLANE), BF),
            pltpu.VMEM((2, CHUNKS, total, CHUNK), BF),
            pltpu.VMEM((ROWS * 2 * KB, 128), F32),
            pltpu.SemaphoreType.DMA,
            pltpu.SemaphoreType.DMA((2, CHUNKS)),
        ],
        compiler_params=pltpu.CompilerParams(vmem_limit_bytes=50 * MIB),
        name="tail_part",
    )(
        first_kz, table_x, received, wave, everything,
    )


def exchange(array):
    return lax.all_to_all(array, "fft", split_axis=0, concat_axis=0, tiled=True)


def on_device(
    wave_coeffs,
    local_potential,
    projector,
    slot_block,
    slot_atom,
    atom_species,
    proj_count,
    projector_strength,
):
    tables = {name: jnp.asarray(value) for name, value in constants().items()}
    rows = wave_coeffs.transpose(1, 0, 2)
    wave = rows.reshape(HD, NBD, 2 * KB, KB)

    projector = projector.reshape(SD, NPROJ, 8, NG).transpose(0, 2, 1, 3).reshape(SD, 64, NG)
    potential = local_potential.reshape(NBLK, 8, NG)
    ids = jnp.concatenate(
        [(slot_atom // 32)[None], (slot_atom % 32)[None], jnp.zeros((14, SD), jnp.int32)]
    ).astype(BF)
    species = jnp.take(atom_species, slot_atom, axis=0)
    kinds = (species[:, None] == jnp.arange(256, dtype=jnp.int32)[None, :] // 64).astype(F32)
    symmetric = 0.5 * (projector_strength + jnp.swapaxes(projector_strength, 1, 2))
    active = (jnp.arange(NPROJ, dtype=jnp.int32)[None, :] < proj_count[:, None]).astype(F32)
    masked = symmetric * active[:, :, None] * active[:, None, :]
    mix = masked.transpose(2, 0, 1)[:, None, :, :, None] * jnp.eye(8, dtype=F32)[None, :, None, None]
    mix = jnp.pad(mix.reshape(64, 256), ((0, 64), (0, 0)))

    sent = x_transform(tables["a"], wave)
    sent, rows = lax.optimization_barrier((sent, rows))
    flat = rows.reshape(ROWS, PLANE)
    everything = lax.all_gather(flat, "band", axis=0, tiled=True)
    prepared = (ids, kinds, mix, projector, potential)
    received = exchange(sent.reshape(ND, DX, LANES)).reshape(ND * DX, LANES)
    received, prepared = lax.optimization_barrier((received, prepared))
    ids, kinds, mix, projector, potential = prepared
    terms, real_space = grid_part(tables, received, projector, slot_block, ids)
    exchanged = exchange(terms)
    sent = apply_part(
        tables, exchanged, ids, kinds, mix, real_space, potential, projector, slot_block
    )
    received = exchange(sent.reshape(ND, DX, LANES)).reshape(ND * DX, LANES)
    first_kz = (lax.axis_index("fft") * HD).astype(jnp.int32).reshape(1)
    result, partial = tail_part(tables["d"], first_kz, received, everything, flat)
    summed = exchange(partial).sum(axis=0) * (1.0 / (KB * KB * KB))
    subspace = summed.reshape(8, 2, 64).transpose(1, 0, 2).reshape(NBD, 4, 64)
    result_coeffs = result.reshape(HD, NBD, PLANE).transpose(1, 0, 2)
    return (result_coeffs, subspace)


def solution(mesh):
    return jax.shard_map(
        on_device,
        mesh=mesh,
        in_specs=(
            P("band", "fft", None),
            P("fft", None),
            P("fft", None, None),
            P("fft"),
            P("fft"),
            P(),
            P(),
            P(),
        ),
        out_specs=(P("band", "fft", None), P("band", None, None)),
        check_vma=False,
    )
```
